32 devices in a mesh: facet: 4 (over y, x), chan: 8 (over z, core).
Axes of the slice: x: 2, y: 2, z: 4, core: 2. Of those that a mesh axis runs over, the one named last changes fastest.
Arguments:
- visibility: float32 [512, 2, 512], P(('facet', 'chan')), may hold values from -6 to 6
- uv_coords: float32 [512, 2, 512], P(('facet', 'chan')), may hold values from 0 to 63
- vis_count: int32 [512], P(('facet', 'chan')), may hold values from 256 to 512, as said below
- subgrid_facet: int32 [512, 1], P(('facet', 'chan')), may hold values from 0 to 3; in each aligned block of 16 rows (0 to 15, 16 to 31, ...) at most 8 rows name the same one
- row_offset: int32 [512], P(('facet', 'chan')), may hold values from 0 to 64
- col_offset: int32 [512], P(('facet', 'chan')), may hold values from 0 to 4032
- model_facet: bfloat16 [4, 128, 2, 4096], P('facet'), may hold values from -6 to 6
Outputs:
- facet_image: float32 [4, 128, 2, 4096], P('facet', 'chan')
- residual_vis: float32 [512, 2, 512], P(('facet', 'chan'))
The draws below stay inside these ranges and needn't reach their ends.
Inputs may be any that keep to these rules, and one draw needn't show every extreme that they name: `subgrid_facet`: in every device's block of 16 subgrids at most 8 name the same facet, a bound that some block reaches. `vis_count`: in every device's block of 16 subgrids one subgrid has all 512 visibilities live.
All inputs are finite; a program needn't handle non-finite values.
Results may differ from the reference program's by a relative error of at most 0.012.
Values may be sent and summed in bfloat16 or wider, within the bound.
No kernel may reach another device: no remote copies, remote signals or barrier semaphores. Data moves between devices by JAX's collectives and lax.ppermute only.
A program may use at most 64 MiB of HBM per device.

```python
import math
import jax
import jax.numpy as jnp
import numpy as np
from jax import lax

SUB = 64
FACET = 4096
F_ROWS = 128
NV = 512
S_DEV = 16
CAP = 8
FACETS = 4
S_TOTAL = 512


def draw_vis_count(key, part):
    block_count = S_TOTAL // S_DEV
    first_key, second_key = jax.random.split(jax.random.fold_in(key, 7))
    base_counts = jax.random.randint(first_key, (block_count, S_DEV), NV // 2, NV + 1)
    peak_index = jax.random.randint(second_key, (block_count, 1), 0, S_DEV)
    filled = jnp.where(jnp.arange(S_DEV)[None, :] == peak_index, NV, base_counts)
    return filled.reshape(S_TOTAL).astype(jnp.int32)


def plant(entries, rng, low, largest):
    dims = entries.shape
    spot = [jax.random.randint(jax.random.fold_in(rng, axis), (), 0, dims[axis]) for axis in range(len(dims))]
    entries = entries.at[tuple(spot)].set(low)
    longest = dims.index(max(dims))
    spot[longest] = (spot[longest] + 1) % dims[longest]
    return entries.at[tuple(spot)].set(largest)


def block_scale(own_key, dims, shards, smallest, largest):
    def one(dim, shards_of):
        draws = jax.random.uniform(jax.random.fold_in(jax.random.fold_in(own_key, 6), dim), (shards_of,), jnp.float32, smallest / len(shards), largest / len(shards))
        return jnp.repeat(jnp.exp(draws), dims[dim] // shards_of).reshape((-1,) + (1,) * (len(dims) - dim - 1))

    loudness = one(*shards[0])
    for cut in shards[1:]:
        loudness = loudness * one(*cut)
    return loudness


def routed_block(key, own, number, rows, count, top, reach, skew):
    sequence = jax.random.permutation(key, count)
    heavy_load, common = load_shares(count, rows * top, reach, skew, True), load_shares(count, rows * top, reach, skew, False)
    places = jnp.arange(count)

    def named(lengths, rotation):
        used = int((lengths > 0).sum())
        fixed = max(1, used // 4)
        moved = fixed + (places - fixed + rotation * (used - fixed)) % max(1, count - fixed)
        return jnp.zeros((count,), jnp.int32).at[sequence[jnp.where(places < fixed, places, moved)]].set(jnp.asarray(lengths, jnp.int32))

    lengths = jnp.where(number % 4 == 0, named(heavy_load, number // 4), named(common, number - number // 4 - 1))
    mixed = jax.random.permutation(jax.random.fold_in(own, 3), count)
    giver, sink = mixed[0:count // 2 * 2:2], mixed[1:count // 2 * 2:2]
    room = jnp.minimum(lengths[giver] - 1, reach - lengths[sink]) // 2
    room = jnp.where((giver == sequence[0]) | (sink == sequence[0]) | (lengths[sink] == 0), 0, jnp.maximum(room, 0))
    moved = jax.random.randint(jax.random.fold_in(own, 4), (count // 2,), 0, 1 << 20) % (room + 1)
    lengths = lengths.at[giver].add(-moved).at[sink].add(moved)
    members = jnp.searchsorted(jnp.cumsum(lengths), jnp.arange(rows * top), side="right").astype(jnp.int32)
    listing = members.reshape(top, rows).T
    listing = listing[jax.random.permutation(jax.random.fold_in(own, 1), rows)]
    rotation = jax.random.randint(jax.random.fold_in(own, 2), (rows, 1), 0, top)
    return jnp.take_along_axis(listing, (jnp.arange(top)[None, :] + rotation) % top, axis=1)


def load_shares(count, total, limit, slope, full):
    portions = [(1 << 20) // math.isqrt(rank ** slope) + 1 for rank in range(1, count + 1)]
    largest = limit if full else min(limit, max(-(-total // count), total * portions[0] // sum(portions)))
    least = 1 if total - largest >= count - 1 else 0
    given, rest = [largest] + [least] * (count - 1), total - largest - least * (count - 1)
    while rest > 0:
        free = [i for i in range(1, count) if given[i] < largest] or [i for i in range(1, count) if given[i] < limit]
        whole, remaining = sum([portions[i] for i in free]), rest
        for i in free:
            addition = min(limit - given[i], max(1, remaining * portions[i] // whole), rest)
            given[i] = given[i] + addition
            rest = rest - addition
    return np.array(given)


def normal_values(key, extent, scale, limit, cuts=(), kind=jnp.bfloat16):
    array = jax.random.normal(key, extent, jnp.float32) * scale
    if len(cuts) > 0:
        array = block_scale(key, extent, cuts, -0.22, 0.18) * array
    return jnp.clip(array, min=-limit, max=limit).astype(kind)


def setup_inputs(seed: int = 0) -> dict:
    key_of = jax.random.split(jax.random.key(seed), 8)
    visibility = normal_values(key_of[0], (S_TOTAL, 2, NV), 1.0, 6.0, ((0, 32),), jnp.float32)
    uv_coords = jnp.clip(63.0 * jax.random.uniform(key_of[1], (S_TOTAL, 2, NV), jnp.float32) ** block_scale(key_of[1], (S_TOTAL, 2, NV), ((0, 32),), -0.2, 0.2), 0.0, 63.0)
    vis_count = draw_vis_count(jax.random.fold_in(key_of[7], 71), 0)
    subgrid_facet_keys = jax.random.split(jax.random.fold_in(key_of[3], 1), S_TOTAL // S_DEV)
    subgrid_facet_turns = jax.random.permutation(jax.random.fold_in(key_of[3], 3), S_TOTAL // S_DEV)
    subgrid_facet = jax.vmap(lambda own, number: routed_block(jax.random.fold_in(key_of[3], 2), own, number, S_DEV, FACETS, 1, CAP, 2))(subgrid_facet_keys, subgrid_facet_turns).reshape((S_TOTAL, 1))
    row_offset = plant(jax.random.randint(key_of[4], (S_TOTAL,), 0, F_ROWS - SUB + 1), jax.random.fold_in(key_of[4], 1), 0, F_ROWS - SUB).astype(jnp.int32)
    col_offset = plant(jax.random.randint(key_of[5], (S_TOTAL,), 0, FACET - SUB + 1), jax.random.fold_in(key_of[5], 1), 0, FACET - SUB).astype(jnp.int32)
    model_facet = normal_values(key_of[6], (FACETS, F_ROWS, 2, FACET), 1.0, 6.0, ((0, 4),))
    return dict(visibility=visibility, uv_coords=uv_coords, vis_count=vis_count, subgrid_facet=subgrid_facet, row_offset=row_offset, col_offset=col_offset, model_facet=model_facet)


KERNEL_COEF = 1.0

def dft_tables(length):
    index_line = jnp.arange(length, dtype=jnp.int32)
    phase = index_line[:, None] * index_line[None, :] % length
    angle = 2.0 * math.pi * phase.astype(jnp.float32) / length
    cos_table = (jnp.cos(angle) / math.sqrt(length)).astype(jnp.bfloat16)
    sin_table = (-jnp.sin(angle) / math.sqrt(length)).astype(jnp.bfloat16)
    right_forward = jnp.concatenate([jnp.concatenate([cos_table, sin_table], 1), jnp.concatenate([-sin_table, cos_table], 1)], 0)
    right_inverse = jnp.concatenate([jnp.concatenate([cos_table, -sin_table], 1), jnp.concatenate([sin_table, cos_table], 1)], 0)
    return (cos_table, sin_table, right_forward, right_inverse)

def swap_halves(values):
    half_width = values.shape[-1] // 2
    return jnp.concatenate([-values[..., half_width:], values[..., :half_width]], -1)

def left_product(table, values):
    return jnp.einsum('ja,sam->sjm', table.astype(jnp.float32), values.astype(jnp.float32))

def forward_transform(sub_grid, tables):
    cos_table, sin_table, right_forward, right_inverse = tables
    half = (left_product(cos_table, sub_grid) + left_product(sin_table, swap_halves(sub_grid))).astype(jnp.bfloat16)
    return jnp.einsum('sjb,bm->sjm', half.astype(jnp.float32), right_forward.astype(jnp.float32)).astype(jnp.bfloat16)

def inverse_transform(sub_grid, tables):
    cos_table, sin_table, right_forward, right_inverse = tables
    half = (left_product(cos_table, sub_grid) - left_product(sin_table, swap_halves(sub_grid))).astype(jnp.bfloat16)
    return jnp.einsum('sjb,bm->sjm', half.astype(jnp.float32), right_inverse.astype(jnp.float32)).astype(jnp.bfloat16)

def kernels(coords):
    pixel_grid = jnp.arange(SUB, dtype=jnp.int32).astype(jnp.float32)
    delta_u = pixel_grid[None, None, :] - coords[:, 0, :, None]
    delta_v = pixel_grid[None, None, :] - coords[:, 1, :, None]
    return (jnp.exp(-KERNEL_COEF * delta_u * delta_u), jnp.exp(-KERNEL_COEF * delta_v * delta_v))

def reference(visibility, uv_coords, vis_count, subgrid_facet, row_offset, col_offset, model_facet):
    tables = dft_tables(SUB)
    block_count = S_TOTAL // S_DEV

    def blocked(values):
        return values.reshape((block_count, S_DEV) + values.shape[1:])
    inputs = (blocked(visibility), blocked(uv_coords), blocked(vis_count), blocked(subgrid_facet[:, 0]), blocked(row_offset), blocked(col_offset))
    two_parts = jnp.arange(2, dtype=jnp.int32)
    pixel_line = jnp.arange(SUB, dtype=jnp.int32)

    def one_block(canvas, block):
        vis_block, coord_block, count_block, facet_ids, row_start, col_start = block
        kernel_u, kernel_v = kernels(coord_block)
        live_mask = (jnp.arange(NV, dtype=jnp.int32)[None, :] < count_block[:, None]).astype(jnp.float32)
        weighted = vis_block * live_mask[:, None, :]
        spread = (jnp.transpose(weighted, (0, 2, 1))[:, :, :, None] * kernel_v[:, :, None, :]).reshape(S_DEV, NV, 2 * SUB).astype(jnp.bfloat16)
        kernel_low = kernel_u.astype(jnp.bfloat16)
        gridded = jnp.einsum('ska,skm->sam', kernel_low.astype(jnp.float32), spread.astype(jnp.float32)).astype(jnp.bfloat16)
        patch = forward_transform(gridded, tables)
        row_index = (row_start[:, None] + pixel_line[None, :]).astype(jnp.int32)
        col_index = (col_start[:, None] + pixel_line[None, :]).astype(jnp.int32)
        where_facet = facet_ids[:, None, None, None]
        where_row = row_index[:, :, None, None]
        where_part = two_parts[None, None, :, None]
        where_col = col_index[:, None, None, :]
        values = patch.astype(jnp.float32).reshape(S_DEV, SUB, 2, SUB)
        canvas = canvas.at[where_facet, where_row, where_part, where_col].add(values)
        picked = model_facet[where_facet, where_row, where_part, where_col].reshape(S_DEV, SUB, 2 * SUB)
        image_grid = inverse_transform(picked, tables)
        degridded = jnp.einsum('ska,sam->skm', kernel_low.astype(jnp.float32), image_grid.astype(jnp.float32)).reshape(S_DEV, NV, 2, SUB)
        predicted = lax.optimization_barrier(jnp.sum(degridded * kernel_v[:, :, None, :], -1))
        residual = (vis_block - jnp.transpose(predicted, (0, 2, 1))) * live_mask[:, None, :]
        return (canvas, residual)
    start_canvas = jnp.zeros((FACETS, F_ROWS, 2, FACET), jnp.float32)
    canvas, residual = lax.scan(one_block, start_canvas, inputs)
    return (canvas, residual.reshape(S_TOTAL, 2, NV))
```

```python
import functools
import math

import jax
import jax.numpy as jnp
import numpy as np
from jax import lax
from jax.experimental import pallas as pl
from jax.experimental.pallas import tpu as pltpu
from jax.sharding import PartitionSpec as P

SUB = 64
FACET = 4096
F_ROWS = 128
NV = 512
LANES = 128
VALID_BIT = 1 << 20
GROUP = 4

VMEM_LIMIT = 48 * 1024 * 1024


def dft_arrays():
    index_line = np.arange(SUB)
    phase = (index_line[:, None] * index_line[None, :]) % SUB
    angle = (2.0 * math.pi * phase / SUB).astype(np.float32)
    cos_table = np.cos(angle) / np.float32(math.sqrt(SUB))
    sin_table = -np.sin(angle) / np.float32(math.sqrt(SUB))
    return cos_table.astype(np.float32), sin_table.astype(np.float32)


def forward_tables():
    cos_table, sin_table = dft_arrays()
    left = np.concatenate([cos_table, sin_table], 1)
    right = np.concatenate(
        [np.concatenate([cos_table, sin_table], 1), np.concatenate([-sin_table, cos_table], 1)], 0
    )
    return jnp.asarray(left, jnp.bfloat16), jnp.asarray(right, jnp.bfloat16)


def inverse_tables():
    cos_table, sin_table = dft_arrays()
    wide = np.zeros((2 * SUB, 2 * F_ROWS), np.float32)
    wide[:SUB, 0 : 2 * SUB : 2] = cos_table
    wide[:SUB, 1 : 2 * SUB : 2] = sin_table
    wide[SUB:, 0 : 2 * SUB : 2] = -sin_table
    wide[SUB:, 1 : 2 * SUB : 2] = cos_table
    right = np.concatenate(
        [np.concatenate([cos_table, -sin_table], 1), np.concatenate([sin_table, cos_table], 1)], 0
    )
    return jnp.asarray(wide, jnp.float32), jnp.asarray(right, jnp.bfloat16)


def gaussian(coord_row):
    pixel = lax.broadcasted_iota(jnp.int32, (SUB, NV), 0).astype(jnp.float32)
    delta = pixel - coord_row
    return jnp.exp(-(delta * delta))


def live_row(count):
    return lax.broadcasted_iota(jnp.int32, (1, NV), 1) < count


def next_slot(facet_ref, used_ref, sub):
    facet = facet_ref[sub]
    slot = used_ref[facet]
    used_ref[facet] = slot + 1
    return facet, slot


def clear_used(used_ref, facets):
    for facet in range(facets):
        used_ref[facet] = 0


def grid_kernel(
    facets, chans, facet_ref, row_ref, count_ref, vis_ref, coord_ref, left_ref, right_ref,
    send_ref, pad_ref, used_ref,
):
    subs = vis_ref.shape[0]
    shard = F_ROWS // chans
    clear_used(used_ref, facets)
    pad_ref[...] = jnp.zeros_like(pad_ref)
    low_lanes = lax.broadcasted_iota(jnp.int32, (SUB, LANES), 1) < SUB

    def one_group(group, carry):
        halves = []
        for member in range(GROUP):
            sub = group * GROUP + member
            kernel_u = gaussian(coord_ref[sub, 0:1, :]).astype(jnp.bfloat16)
            kernel_v = gaussian(coord_ref[sub, 1:2, :])
            live = live_row(count_ref[sub])
            spread = jnp.concatenate(
                [
                    (jnp.where(live, vis_ref[sub, part : part + 1, :], 0.0) * kernel_v).astype(
                        jnp.bfloat16
                    )
                    for part in range(2)
                ],
                0,
            )
            gridded = lax.dot_general(
                kernel_u, spread, (((1,), (1,)), ((), ())), preferred_element_type=jnp.float32
            )
            swapped = pltpu.roll(gridded, SUB, 1)
            swapped = jnp.where(low_lanes, -swapped, swapped)
            stacked = jnp.concatenate([gridded, swapped], 0).astype(jnp.bfloat16)
            halves.append(
                jnp.dot(left_ref[...], stacked, preferred_element_type=jnp.float32).astype(
                    jnp.bfloat16
                )
            )
        patches = jnp.dot(
            jnp.concatenate(halves, 0), right_ref[...], preferred_element_type=jnp.float32
        )
        for member in range(GROUP):
            pad_ref[member, SUB : 2 * SUB, :] = patches[member * SUB : (member + 1) * SUB]
        for member in range(GROUP):
            sub = group * GROUP + member
            facet, slot = next_slot(facet_ref, used_ref, sub)
            placed = pad_ref[member, pl.ds(SUB - row_ref[sub], F_ROWS), :].astype(jnp.bfloat16)
            send_ref[pl.ds(facet * chans, chans), slot] = placed.reshape(chans, shard, LANES)
        return carry

    lax.fori_loop(0, subs // GROUP, one_group, 0)


def pick_kernel(
    facets, cap, chan_ref, meta_ref, model_ref, wide_ref, right_ref, back_ref, list_ref
):
    chans = meta_ref.shape[0] // (facets * cap)
    chan = chan_ref[0]

    def note(index, found):
        source = index // cap
        packed = meta_ref[(source * chans + chan) * cap + index % cap]
        list_ref[found] = packed * (facets * cap) + index
        return found + (packed >= VALID_BIT).astype(jnp.int32)

    found = lax.fori_loop(0, facets * cap, note, 0)
    lanes = lax.broadcasted_iota(jnp.int32, (SUB, LANES), 1)

    def handle(position):
        entry = list_ref[position]
        index = entry % (facets * cap)
        packed = entry // (facets * cap)
        row = (packed >> 12) & (LANES - 1)
        col = packed & (FACET - 1)
        block = jnp.minimum(col // LANES, FACET // LANES - 2)
        shift = col - block * LANES
        table = pltpu.roll(wide_ref[...], 2 * row, 1).astype(jnp.bfloat16)
        slab = model_ref[:, pl.ds(pl.multiple_of(block * LANES, LANES), 2 * LANES)]
        half = jnp.dot(table, slab, preferred_element_type=jnp.float32)
        real = pltpu.roll(half[:SUB], lax.rem(2 * LANES - shift, 2 * LANES), 1)[:, :LANES]
        imag = pltpu.roll(half[SUB:], lax.rem(2 * LANES + SUB - shift, 2 * LANES), 1)[:, :LANES]
        window = jnp.where(lanes < SUB, real, imag).astype(jnp.bfloat16)
        image = jnp.dot(window, right_ref[...], preferred_element_type=jnp.float32)
        back_ref[index] = image.astype(jnp.bfloat16)

    def one_group(group, carry):
        for member in range(GROUP):
            handle(jnp.minimum(group * GROUP + member, found - 1))
        return carry

    lax.fori_loop(0, (found + GROUP - 1) // GROUP, one_group, 0)


def add_kernel(chans, chan_ref, meta_ref, recv_ref, image_ref, canvas_ref, list_ref):
    shard = F_ROWS // chans
    slots = meta_ref.shape[0]
    first_row = chan_ref[0] * shard
    canvas_ref[...] = jnp.zeros_like(canvas_ref)

    def note(index, found):
        packed = meta_ref[index]
        row = (packed >> 12) & (LANES - 1)
        keep = (packed >= VALID_BIT) & (row < first_row + shard) & (row + SUB > first_row)
        list_ref[found] = index
        return found + keep.astype(jnp.int32)

    found = lax.fori_loop(0, slots, note, 0)
    lanes = lax.broadcasted_iota(jnp.int32, (shard, LANES), 1)

    def load(position):
        index = list_ref[position]
        col = meta_ref[index] & (FACET - 1)
        start = pl.multiple_of(col // LANES * LANES, LANES)
        shift = lax.rem(col, LANES)
        values = recv_ref[index].astype(jnp.float32)
        real = pltpu.roll(jnp.where(lanes < SUB, values, 0.0), shift, 1)
        imag = pltpu.roll(jnp.where(lanes < SUB, 0.0, values), lax.rem(shift + SUB, LANES), 1)
        high = lanes >= shift
        return start, (
            (0, 0, jnp.where(high, real, 0.0)),
            (0, 1, jnp.where(high, 0.0, real)),
            (1, 0, jnp.where(high, imag, 0.0)),
            (1, 1, jnp.where(high, 0.0, imag)),
        )

    def store(start, pieces):
        for part, block, piece in pieces:
            place = pl.ds(pl.multiple_of(start + block * LANES, LANES), LANES)
            canvas_ref[part, :, place] += piece

    def one_group(group, carry):
        for loaded in [load(group * GROUP + member) for member in range(GROUP)]:
            store(*loaded)
        return carry

    def one(position, carry):
        store(*load(position))
        return carry

    whole = found // GROUP
    lax.fori_loop(0, whole, one_group, 0)
    lax.fori_loop(whole * GROUP, found, one, 0)
    for part in range(2):
        image_ref[:, part, :] = canvas_ref[part, :, :FACET]


def degrid_kernel(
    facets, facet_ref, count_ref, vis_ref, coord_ref, back_ref, out_ref, used_ref
):
    subs = vis_ref.shape[0]
    clear_used(used_ref, facets)
    low_lanes = lax.broadcasted_iota(jnp.int32, (SUB, LANES), 1) < SUB

    def one_group(group, carry):
        for member in range(GROUP):
            sub = group * GROUP + member
            facet, slot = next_slot(facet_ref, used_ref, sub)
            kernel_u = gaussian(coord_ref[sub, 0:1, :]).astype(jnp.bfloat16).astype(jnp.float32)
            kernel_v = gaussian(coord_ref[sub, 1:2, :]).astype(jnp.bfloat16)
            grid = back_ref[facet, slot].astype(jnp.float32)
            split = jnp.concatenate(
                [jnp.where(low_lanes, grid, 0.0), jnp.where(low_lanes, 0.0, grid)], 0
            ).astype(jnp.bfloat16)
            lines = jnp.dot(
                split,
                jnp.concatenate([kernel_v, kernel_v], 0),
                preferred_element_type=jnp.float32,
            )
            live = live_row(count_ref[sub])
            for part in range(2):
                predicted = jnp.sum(
                    lines[part * SUB : (part + 1) * SUB] * kernel_u, 0, keepdims=True
                )
                seen = vis_ref[sub, part : part + 1, :]
                out_ref[sub, part : part + 1, :] = jnp.where(live, seen - predicted, 0.0)
        return carry

    lax.fori_loop(0, subs // GROUP, one_group, 0)


def smem():
    return pl.BlockSpec(memory_space=pltpu.SMEM)


def vmem():
    return pl.BlockSpec(memory_space=pltpu.VMEM)


def params():
    return pltpu.CompilerParams(vmem_limit_bytes=VMEM_LIMIT)


def per_device(
    visibility, uv_coords, vis_count, subgrid_facet, row_offset, col_offset, model_facet
):
    facets = lax.axis_size("facet")
    chans = lax.axis_size("chan")
    subs = visibility.shape[0]
    cap = max(2, 2 * subs // facets)
    shard = F_ROWS // chans
    facet_ids = subgrid_facet[:, 0]
    my_chan = lax.axis_index("chan").astype(jnp.int32).reshape(1)

    packed = VALID_BIT + (row_offset << 12) + col_offset
    order = jnp.arange(subs, dtype=jnp.int32)
    same = facet_ids[:, None] == facet_ids[None, :]
    rank = jnp.sum((same & (order[None, :] < order[:, None])).astype(jnp.int32), 1)
    place = facet_ids * cap + rank
    hit = place[None, :] == jnp.arange(facets * cap, dtype=jnp.int32)[:, None]
    slot_meta = jnp.sum(jnp.where(hit, packed[None, :], 0), 1).reshape(facets, 1, cap)
    send_meta = jnp.broadcast_to(slot_meta, (facets, chans, cap)).reshape(facets * chans, cap)
    recv_meta = lax.all_to_all(
        send_meta, ("facet", "chan"), split_axis=0, concat_axis=0, tiled=True
    ).reshape(-1)

    left, right = forward_tables()
    send = pl.pallas_call(
        functools.partial(grid_kernel, facets, chans),
        out_shape=jax.ShapeDtypeStruct((facets * chans, cap, shard, LANES), jnp.bfloat16),
        in_specs=[smem()] * 3 + [vmem()] * 4,
        out_specs=vmem(),
        scratch_shapes=[
            pltpu.VMEM((GROUP, 3 * SUB, LANES), jnp.float32),
            pltpu.SMEM((facets,), jnp.int32),
        ],
        compiler_params=params(),
        name="grid",
    )(facet_ids, row_offset, vis_count, visibility, uv_coords, left, right)
    recv = lax.all_to_all(send, ("facet", "chan"), split_axis=0, concat_axis=0, tiled=True)

    wide, inverse = inverse_tables()
    model = model_facet.reshape(2 * F_ROWS, FACET)
    back = pl.pallas_call(
        functools.partial(pick_kernel, facets, cap),
        out_shape=jax.ShapeDtypeStruct((facets * cap, SUB, LANES), jnp.bfloat16),
        in_specs=[smem()] * 2 + [vmem()] * 3,
        out_specs=vmem(),
        scratch_shapes=[pltpu.SMEM((facets * cap + 1,), jnp.int32)],
        compiler_params=params(),
        name="pick",
    )(my_chan, recv_meta, model, wide, inverse)
    returned = lax.all_to_all(
        back.reshape(facets, cap, SUB, LANES), "facet", split_axis=0, concat_axis=0, tiled=True
    )

    residual_vis = pl.pallas_call(
        functools.partial(degrid_kernel, facets),
        out_shape=jax.ShapeDtypeStruct((subs, 2, NV), jnp.float32),
        in_specs=[smem()] * 2 + [vmem()] * 3,
        out_specs=vmem(),
        scratch_shapes=[pltpu.SMEM((facets,), jnp.int32)],
        compiler_params=params(),
        name="degrid",
    )(facet_ids, vis_count, visibility, uv_coords, returned)

    slots = facets * chans * cap
    facet_image = pl.pallas_call(
        functools.partial(add_kernel, chans),
        out_shape=jax.ShapeDtypeStruct((shard, 2, FACET), jnp.float32),
        in_specs=[smem()] * 2 + [vmem()],
        out_specs=vmem(),
        scratch_shapes=[
            pltpu.VMEM((2, shard, FACET + LANES), jnp.float32),
            pltpu.SMEM((slots + 1,), jnp.int32),
        ],
        compiler_params=params(),
        name="add",
    )(my_chan, recv_meta, recv.reshape(slots, shard, LANES))
    return (facet_image[None], residual_vis)


def solution(mesh):
    in_specs = (
        P(("facet", "chan"), None, None),
        P(("facet", "chan"), None, None),
        P(("facet", "chan")),
        P(("facet", "chan"), None),
        P(("facet", "chan")),
        P(("facet", "chan")),
        P("facet", None, None, None),
    )
    out_specs = (P("facet", "chan", None, None), P(("facet", "chan"), None, None))
    return jax.shard_map(
        per_device, mesh=mesh, in_specs=in_specs, out_specs=out_specs, check_vma=False
    )
```

```python
import functools
import math

import jax
import jax.numpy as jnp
import numpy as np
from jax import lax
from jax.experimental import pallas as pl
from jax.experimental.pallas import tpu as pltpu
from jax.sharding import PartitionSpec as P

SUB = 64
FACET = 4096
F_ROWS = 128
NV = 512
LANES = 128
VALID_BIT = 1 << 20
GROUP = 4
WORDS = 128
COUNTS = 32
PLACE = 64

SPAN = 3 * SUB
TRASH = 2 * FACET
ADD_GROUP = 8
PICK_GROUP = 8
CANVASES = 4

VMEM_LIMIT = 48 * 1024 * 1024


def dft_arrays():
    index_line = np.arange(SUB)
    phase = (index_line[:, None] * index_line[None, :]) % SUB
    angle = (2.0 * math.pi * phase / SUB).astype(np.float32)
    cos_table = np.cos(angle) / np.float32(math.sqrt(SUB))
    sin_table = -np.sin(angle) / np.float32(math.sqrt(SUB))
    return cos_table.astype(np.float32), sin_table.astype(np.float32)


def forward_table():
    cos_table, sin_table = dft_arrays()
    right = np.concatenate(
        [np.concatenate([cos_table, sin_table], 1), np.concatenate([-sin_table, cos_table], 1)], 0
    )
    return jnp.asarray(right, jnp.bfloat16)


def inverse_tables():
    cos_table, sin_table = dft_arrays()
    sin_table = -sin_table
    columns = np.zeros((2 * SPAN + SUB, LANES), np.float32)
    columns[SPAN : SPAN + SUB] = np.concatenate([cos_table, sin_table], 1)
    rows = np.zeros((2 * SUB, 2 * SUB), np.float32)
    rows[:SUB, 0::2] = cos_table
    rows[:SUB, 1::2] = -sin_table
    rows[SUB:, 0::2] = sin_table
    rows[SUB:, 1::2] = cos_table
    columns = columns.astype(jnp.bfloat16).astype(np.float32)
    return jnp.asarray(columns), jnp.asarray(rows, jnp.bfloat16)


def gaussian(coord_row):
    pixel = lax.broadcasted_iota(jnp.int32, (SUB, NV), 0).astype(jnp.float32)
    delta = pixel - coord_row
    return jnp.exp(-(delta * delta))


def live_row(count):
    return lax.broadcasted_iota(jnp.int32, (1, NV), 1) < count


def fetch(copies, sems):
    started = [
        pltpu.make_async_copy(source, target, sems.at[number])
        for number, (source, target) in enumerate(copies)
    ]
    for copy in started:
        copy.start()
    for copy in started:
        copy.wait()


def facet_of(meta_ref, sub):
    return lax.div(meta_ref[sub], F_ROWS * FACET)


def row_of(meta_ref, sub):
    return lax.div(meta_ref[sub], FACET) & (F_ROWS - 1)


def count_of(meta_ref, sub):
    return meta_ref[COUNTS + sub]


def next_slot(meta_ref, used_ref, sub):
    facet = facet_of(meta_ref, sub)
    slot = used_ref[facet]
    used_ref[facet] = slot + 1
    return facet, slot


def clear_used(used_ref, facets):
    for facet in range(facets):
        used_ref[facet] = 0


def grid_kernel(
    facets, chans, meta_in, vis_in, coord_in, right_in, send_ref,
    meta_ref, vis_ref, coord_ref, right_ref, stack_ref, half_ref, pad_ref, used_ref, sems,
):
    subs = vis_ref.shape[0]
    shard = F_ROWS // chans
    fetch(
        [
            (meta_in, meta_ref),
            (vis_in, vis_ref),
            (coord_in, coord_ref),
            (right_in, right_ref),
        ],
        sems,
    )
    clear_used(used_ref, facets)
    for member in range(GROUP):
        pad_ref[member, :SUB, :] = jnp.zeros((SUB, LANES), jnp.float32)
        pad_ref[member, 2 * SUB :, :] = jnp.zeros((SUB, LANES), jnp.float32)
    low_lanes = lax.broadcasted_iota(jnp.int32, (SUB, LANES), 1) < SUB

    def grid_one(sub):
        kernel_u = gaussian(coord_ref[sub, 0:1, :]).astype(jnp.bfloat16)
        kernel_v = gaussian(coord_ref[sub, 1:2, :])
        live = live_row(count_of(meta_ref, sub))
        spread = jnp.concatenate(
            [
                (jnp.where(live, vis_ref[sub, part : part + 1, :], 0.0) * kernel_v).astype(
                    jnp.bfloat16
                )
                for part in range(2)
            ],
            0,
        )
        gridded = lax.dot_general(
            kernel_u, spread, (((1,), (1,)), ((), ())), preferred_element_type=jnp.float32
        )
        swapped = pltpu.roll(gridded, SUB, 1)
        swapped = jnp.where(low_lanes, -swapped, swapped)
        stack_ref[sub] = jnp.concatenate([gridded, swapped], 0).astype(jnp.bfloat16)

    def grid_group(group, carry):
        for member in range(GROUP):
            grid_one(group * GROUP + member)
        return carry

    lax.fori_loop(0, subs // GROUP, grid_group, 0)
    for sub in range(subs):
        half_ref[sub * SUB : (sub + 1) * SUB, :] = jnp.dot(
            right_ref[:SUB, :], stack_ref[sub], preferred_element_type=jnp.float32
        ).astype(jnp.bfloat16)

    for group in range(subs // GROUP):
        base = group * GROUP
        patches = jnp.dot(
            half_ref[base * SUB : (base + GROUP) * SUB, :],
            right_ref[...],
            preferred_element_type=jnp.float32,
        )
        for member in range(GROUP):
            pad_ref[member, SUB : 2 * SUB, :] = patches[member * SUB : (member + 1) * SUB]
        for member in range(GROUP):
            sub = base + member
            facet, slot = next_slot(meta_ref, used_ref, sub)
            placed = pad_ref[member, pl.ds(SUB - row_of(meta_ref, sub), F_ROWS), :].astype(jnp.bfloat16)
            send_ref[pl.ds(facet * chans, chans), slot] = placed.reshape(chans, shard, LANES)


def pick_kernel(facets, subs, cap, *refs):
    meta_in, refs = refs[:facets], refs[facets:]
    model_ref, columns_ref, rows_ref, *refs = refs
    back_out, refs = refs[:facets], refs[facets:]
    mine_ref, meta_ref, back_ref, list_ref, sems, out_sems, *wide_refs = refs
    slots = facets * cap
    fetch(
        [
            (meta_in[number], meta_ref.at[pl.ds(number * WORDS, WORDS)])
            for number in range(facets)
        ],
        sems,
    )
    facet = meta_ref[PLACE]
    for index in range(slots):
        mine_ref[index] = 0
    found = 0
    base = facet * (F_ROWS * FACET)
    for source in range(facets):
        slot = source * cap
        for sub in range(subs):
            where = meta_ref[source * WORDS + sub] - base
            hit = (where >= 0) & (where < F_ROWS * FACET)
            mine_ref[jnp.where(hit, slot, slots)] = where + VALID_BIT
            list_ref[found] = where * slots + slot
            slot = slot + hit.astype(jnp.int32)
            found = found + hit.astype(jnp.int32)

    low_lanes = lax.broadcasted_iota(jnp.int32, (SUB, LANES), 1) < SUB

    def columns_of(position, wide_ref):
        entry = list_ref[position]
        where = lax.div(entry, slots)
        col = where & (FACET - 1)
        block = jnp.minimum(lax.div(col, LANES), FACET // LANES - 2)
        slab = model_ref[:, pl.ds(pl.multiple_of(block * LANES, LANES), 2 * LANES)]
        table = columns_ref[pl.ds(SPAN - col + block * LANES, 2 * LANES), :]
        wide_ref[...] = jnp.dot(
            slab, table.astype(jnp.bfloat16), preferred_element_type=jnp.float32
        )
        return lax.rem(entry, slots), lax.div(where, FACET)

    def rows_of(row, wide_ref):
        half = wide_ref[pl.ds(2 * row, 2 * SUB), :].astype(jnp.bfloat16)
        return jnp.dot(rows_ref[...], half, preferred_element_type=jnp.float32)

    def finish(image):
        turned = pltpu.roll(image[SUB:], SUB, 1)
        return (image[:SUB] + jnp.where(low_lanes, -turned, turned)).astype(jnp.bfloat16)

    def one_group(group, carry):
        places = [
            columns_of(jnp.minimum(group * PICK_GROUP + member, found - 1), wide_refs[member])
            for member in range(PICK_GROUP)
        ]
        images = [rows_of(row, wide_refs[member]) for member, (_, row) in enumerate(places)]
        images = [finish(image) for image in images]
        for (index, _), image in zip(places, images):
            back_ref[index] = image
        return carry

    lax.fori_loop(0, lax.div(found + PICK_GROUP - 1, PICK_GROUP), one_group, 0)
    fetch(
        [
            (back_ref.at[pl.ds(number * cap, cap)], back_out[number])
            for number in range(facets)
        ],
        out_sems,
    )


def list_kernel(facets, chans, cap, place_ref, meta_ref, list_ref):
    shard = F_ROWS // chans
    facet, chan = place_ref[PLACE], place_ref[PLACE + 1]
    first_row = chan * shard
    total = facets * chans * cap
    low, high = (first_row - SUB + 1) * FACET, (first_row + shard) * FACET

    def one_source(source, found):
        source_facet = (source & (facets - 1)) ^ facet
        source_chan = lax.div(source, facets) ^ chan
        first_slot = (source_facet * chans + source_chan) * cap
        values = [meta_ref[source * cap + slot] for slot in range(cap)]
        for slot, packed in enumerate(values):
            where = packed - VALID_BIT
            keep = (where >= jnp.maximum(low, 0)) & (where < high)
            list_ref[found] = (first_slot + slot) * TRASH + (packed & (FACET - 1))
            found = found + keep.astype(jnp.int32)
        return found

    found = lax.fori_loop(0, facets * chans, one_source, 0)
    for member in range(ADD_GROUP):
        list_ref[found + member] = FACET + LANES
    list_ref[total + ADD_GROUP] = lax.div(found + ADD_GROUP - 1, ADD_GROUP)


def add_kernel(chans, list_ref, recv_ref, image_ref, *canvas_refs):
    shard = F_ROWS // chans
    slots = recv_ref.shape[0]
    for canvas_ref in canvas_refs:
        canvas_ref[...] = jnp.zeros_like(canvas_ref)
    lanes = lax.broadcasted_iota(jnp.int32, (shard, LANES), 1)

    def load(position):
        entry = list_ref[position]
        col = entry & (TRASH - 1)
        start = pl.multiple_of(lax.div(col, LANES) * LANES, LANES)
        shift = col & (LANES - 1)
        values = recv_ref[lax.div(entry, TRASH)].astype(jnp.float32)
        real = pltpu.roll(jnp.where(lanes < SUB, values, 0.0), shift, 1)
        imag = pltpu.roll(jnp.where(lanes < SUB, 0.0, values), (shift + SUB) & (LANES - 1), 1)
        return start, lanes >= shift, real, imag

    def store(canvas_ref, start, high, real, imag):
        near = pl.ds(start, LANES)
        far = pl.ds(pl.multiple_of(start + LANES, LANES), LANES)
        canvas_ref[0, :, near] += jnp.where(high, real, 0.0)
        canvas_ref[0, :, far] += jnp.where(high, 0.0, real)
        canvas_ref[1, :, near] += jnp.where(high, imag, 0.0)
        canvas_ref[1, :, far] += jnp.where(high, 0.0, imag)

    def one_group(group, carry):
        loaded = [load(group * ADD_GROUP + member) for member in range(ADD_GROUP)]
        for member, values in enumerate(loaded):
            store(canvas_refs[member % CANVASES], *values)
        return carry

    lax.fori_loop(0, list_ref[slots + ADD_GROUP], one_group, 0)
    for part in range(2):
        image_ref[:, part, :] = sum(ref[part, :, :FACET] for ref in canvas_refs)


def degrid_kernel(facets, meta_ref, vis_ref, coord_ref, *refs):
    back_in, refs = refs[:facets], refs[facets:]
    out_ref, back_ref, used_ref, sems = refs
    subs = vis_ref.shape[0]
    fetch([(back_in[number], back_ref.at[number]) for number in range(facets)], sems)
    me = meta_ref[PLACE]
    clear_used(used_ref, facets)
    low_lanes = lax.broadcasted_iota(jnp.int32, (SUB, LANES), 1) < SUB

    def one_group(group, carry):
        for member in range(GROUP):
            sub = group * GROUP + member
            facet, slot = next_slot(meta_ref, used_ref, sub)
            kernel_u = gaussian(coord_ref[sub, 0:1, :]).astype(jnp.bfloat16).astype(jnp.float32)
            kernel_v = gaussian(coord_ref[sub, 1:2, :]).astype(jnp.bfloat16)
            grid = back_ref[facet ^ me, slot].astype(jnp.float32)
            split = jnp.concatenate(
                [jnp.where(low_lanes, grid, 0.0), jnp.where(low_lanes, 0.0, grid)], 0
            ).astype(jnp.bfloat16)
            lines = jnp.dot(
                split,
                jnp.concatenate([kernel_v, kernel_v], 0),
                preferred_element_type=jnp.float32,
            )
            live = live_row(count_of(meta_ref, sub))
            for part in range(2):
                predicted = jnp.sum(
                    lines[part * SUB : (part + 1) * SUB] * kernel_u, 0, keepdims=True
                )
                seen = vis_ref[sub, part : part + 1, :]
                out_ref[sub, part : part + 1, :] = jnp.where(live, seen - predicted, 0.0)
        return carry

    lax.fori_loop(0, subs // GROUP, one_group, 0)


def smem():
    return pl.BlockSpec(memory_space=pltpu.SMEM)


def vmem():
    return pl.BlockSpec(memory_space=pltpu.VMEM)


def hbm():
    return pl.BlockSpec(memory_space=pltpu.HBM)


def params():
    return pltpu.CompilerParams(vmem_limit_bytes=VMEM_LIMIT)


def copy_sems(count):
    return pltpu.SemaphoreType.DMA((count,))


def partner(values, axis, bit):
    return lax.ppermute(
        values, axis, [(index, index ^ bit) for index in range(lax.axis_size(axis))]
    )


def per_device(
    visibility, uv_coords, vis_count, subgrid_facet, row_offset, col_offset, model_facet
):
    facets = lax.axis_size("facet")
    chans = lax.axis_size("chan")
    subs = visibility.shape[0]
    cap = max(2, 2 * subs // facets)
    shard = F_ROWS // chans
    slots = facets * cap
    total = slots * chans
    facet_ids = subgrid_facet[:, 0]
    zeros = jnp.zeros((COUNTS - subs,), jnp.int32)
    meta = jnp.concatenate(
        [
            (facet_ids * F_ROWS + row_offset) * FACET + col_offset,
            zeros,
            vis_count,
            zeros,
            lax.axis_index("facet").astype(jnp.int32).reshape(1),
            lax.axis_index("chan").astype(jnp.int32).reshape(1),
            jnp.zeros((WORDS - PLACE - 2,), jnp.int32),
        ]
    )
    metas = [meta] + [partner(meta, "facet", bit) for bit in range(1, facets)]

    send = pl.pallas_call(
        functools.partial(grid_kernel, facets, chans),
        out_shape=jax.ShapeDtypeStruct((facets * chans, cap, shard, LANES), jnp.bfloat16),
        in_specs=[hbm()] * 4,
        out_specs=vmem(),
        scratch_shapes=[
            pltpu.SMEM((WORDS,), jnp.int32),
            pltpu.VMEM((subs, 2, NV), jnp.float32),
            pltpu.VMEM((subs, 2, NV), jnp.float32),
            pltpu.VMEM((LANES, LANES), jnp.bfloat16),
            pltpu.VMEM((subs, LANES, LANES), jnp.bfloat16),
            pltpu.VMEM((subs * SUB, LANES), jnp.bfloat16),
            pltpu.VMEM((GROUP, 3 * SUB, LANES), jnp.float32),
            pltpu.SMEM((facets,), jnp.int32),
            copy_sems(4),
        ],
        compiler_params=params(),
        name="grid",
    )(meta, visibility, uv_coords, forward_table())
    send, model_facet = lax.optimization_barrier((send, model_facet))
    recv = lax.all_to_all(send, ("facet", "chan"), split_axis=0, concat_axis=0, tiled=True)

    columns, rows = inverse_tables()
    model = model_facet.reshape(2 * F_ROWS, FACET)
    picked = pl.pallas_call(
        functools.partial(pick_kernel, facets, subs, cap),
        out_shape=tuple(
            [jax.ShapeDtypeStruct((cap, SUB, LANES), jnp.bfloat16)] * facets
            + [jax.ShapeDtypeStruct((WORDS,), jnp.int32)]
        ),
        in_specs=[hbm()] * facets + [vmem()] * 3,
        out_specs=tuple([hbm()] * facets + [smem()]),
        scratch_shapes=[
            pltpu.SMEM((facets * WORDS,), jnp.int32),
            pltpu.VMEM((slots, SUB, LANES), jnp.bfloat16),
            pltpu.SMEM((slots + 1,), jnp.int32),
            copy_sems(facets),
            copy_sems(facets),
        ]
        + [pltpu.VMEM((2 * F_ROWS, LANES), jnp.float32)] * PICK_GROUP,
        compiler_params=params(),
        name="pick",
    )(*metas, model, columns, rows)
    back, mine = picked[:facets], picked[facets][:slots]
    returned = [back[0]] + [partner(back[bit], "facet", bit) for bit in range(1, facets)]

    bit = 1
    while bit < chans:
        mine = jnp.concatenate([mine, partner(mine, "chan", bit)])
        bit *= 2
    entries = pl.pallas_call(
        functools.partial(list_kernel, facets, chans, cap),
        out_shape=jax.ShapeDtypeStruct((total + ADD_GROUP + 1,), jnp.int32),
        in_specs=[smem()] * 2,
        out_specs=smem(),
        compiler_params=params(),
        name="entries",
    )(meta, mine)

    residual_vis = pl.pallas_call(
        functools.partial(degrid_kernel, facets),
        out_shape=jax.ShapeDtypeStruct((subs, 2, NV), jnp.float32),
        in_specs=[smem()] + [vmem()] * 2 + [hbm()] * facets,
        out_specs=vmem(),
        scratch_shapes=[
            pltpu.VMEM((facets, cap, SUB, LANES), jnp.bfloat16),
            pltpu.SMEM((facets,), jnp.int32),
            copy_sems(facets),
        ],
        compiler_params=params(),
        name="degrid",
    )(meta, visibility, uv_coords, *returned)

    facet_image = pl.pallas_call(
        functools.partial(add_kernel, chans),
        out_shape=jax.ShapeDtypeStruct((shard, 2, FACET), jnp.float32),
        in_specs=[smem(), vmem()],
        out_specs=vmem(),
        scratch_shapes=[pltpu.VMEM((2, shard, FACET + 3 * LANES), jnp.float32)] * CANVASES,
        compiler_params=params(),
        name="add",
    )(entries, recv.reshape(total, shard, LANES))
    return (facet_image[None], residual_vis)


def solution(mesh):
    in_specs = (
        P(("facet", "chan"), None, None),
        P(("facet", "chan"), None, None),
        P(("facet", "chan")),
        P(("facet", "chan"), None),
        P(("facet", "chan")),
        P(("facet", "chan")),
        P("facet", None, None, None),
    )
    out_specs = (P("facet", "chan", None, None), P(("facet", "chan"), None, None))
    return jax.shard_map(
        per_device, mesh=mesh, in_specs=in_specs, out_specs=out_specs, check_vma=False
    )
```

```python
import functools
import math

import jax
import jax.numpy as jnp
import numpy as np
from jax import lax
from jax.experimental import pallas as pl
from jax.experimental.pallas import tpu as pltpu
from jax.sharding import PartitionSpec as P

SUB = 64
FACET = 4096
F_ROWS = 128
NV = 512
LANES = 128
VALID_BIT = 1 << 20
GROUP = 4
WORDS = 128

SPAN = 3 * SUB
PICK_GROUP = 8
CANVASES = 4

VMEM_LIMIT = 48 * 1024 * 1024


def dft_arrays():
    index_line = np.arange(SUB)
    phase = (index_line[:, None] * index_line[None, :]) % SUB
    angle = (2.0 * math.pi * phase / SUB).astype(np.float32)
    cos_table = np.cos(angle) / np.float32(math.sqrt(SUB))
    sin_table = -np.sin(angle) / np.float32(math.sqrt(SUB))
    return cos_table.astype(np.float32), sin_table.astype(np.float32)


def forward_table():
    cos_table, sin_table = dft_arrays()
    right = np.concatenate(
        [np.concatenate([cos_table, sin_table], 1), np.concatenate([-sin_table, cos_table], 1)], 0
    )
    return jnp.asarray(right, jnp.bfloat16)


def inverse_tables():
    cos_table, sin_table = dft_arrays()
    sin_table = -sin_table
    columns = np.zeros((2 * SPAN + SUB, LANES), np.float32)
    columns[SPAN : SPAN + SUB] = np.concatenate([cos_table, sin_table], 1)
    rows = np.zeros((2 * SUB, 2 * SUB), np.float32)
    rows[:SUB, 0::2] = cos_table
    rows[:SUB, 1::2] = -sin_table
    rows[SUB:, 0::2] = sin_table
    rows[SUB:, 1::2] = cos_table
    columns = columns.astype(jnp.bfloat16).astype(np.float32)
    return jnp.asarray(columns), jnp.asarray(rows, jnp.bfloat16)


def gaussian(coord_row):
    pixel = lax.broadcasted_iota(jnp.int32, (SUB, NV), 0).astype(jnp.float32)
    delta = pixel - coord_row
    return jnp.exp(-(delta * delta))


def live_row(count):
    return lax.broadcasted_iota(jnp.int32, (1, NV), 1) < count


def fetch(copies, sems):
    started = [
        pltpu.make_async_copy(source, target, sems.at[number])
        for number, (source, target) in enumerate(copies)
    ]
    for copy in started:
        copy.start()
    for copy in started:
        copy.wait()


def next_slot(facet_ref, used_ref, sub):
    facet = facet_ref[sub]
    slot = used_ref[facet]
    used_ref[facet] = slot + 1
    return facet, slot


def clear_used(used_ref, facets):
    for facet in range(facets):
        used_ref[facet] = 0


def grid_kernel(
    facets, chans, facet_in, row_in, col_in, count_in, vis_in, coord_in, right_in, send_ref, *refs
):
    meta_refs, refs = refs[:facets], refs[facets:]
    facet_ref, row_ref, col_ref, count_ref, vis_ref, coord_ref, right_ref, *refs = refs
    stack_ref, half_ref, pad_ref, used_ref, where_ref, sems = refs
    me = lax.axis_index("facet")
    cap = send_ref.shape[1]
    subs = vis_ref.shape[0]
    shard = F_ROWS // chans
    fetch(
        [
            (facet_in, facet_ref),
            (row_in, row_ref),
            (col_in, col_ref),
            (count_in, count_ref),
            (vis_in, vis_ref),
            (coord_in, coord_ref),
            (right_in, right_ref),
        ],
        sems,
    )
    clear_used(used_ref, facets)
    for index in range(facets * cap):
        where_ref[index] = 0
    for member in range(GROUP):
        pad_ref[member, :SUB, :] = jnp.zeros((SUB, LANES), jnp.float32)
        pad_ref[member, 2 * SUB :, :] = jnp.zeros((SUB, LANES), jnp.float32)
    low_lanes = lax.broadcasted_iota(jnp.int32, (SUB, LANES), 1) < SUB

    def grid_one(sub):
        kernel_u = gaussian(coord_ref[sub, 0:1, :]).astype(jnp.bfloat16)
        kernel_v = gaussian(coord_ref[sub, 1:2, :])
        live = live_row(count_ref[sub])
        spread = jnp.concatenate(
            [
                (jnp.where(live, vis_ref[sub, part : part + 1, :], 0.0) * kernel_v).astype(
                    jnp.bfloat16
                )
                for part in range(2)
            ],
            0,
        )
        gridded = lax.dot_general(
            kernel_u, spread, (((1,), (1,)), ((), ())), preferred_element_type=jnp.float32
        )
        swapped = pltpu.roll(gridded, SUB, 1)
        swapped = jnp.where(low_lanes, -swapped, swapped)
        stack_ref[sub] = jnp.concatenate([gridded, swapped], 0).astype(jnp.bfloat16)

    def grid_group(group, carry):
        for member in range(GROUP):
            grid_one(group * GROUP + member)
        return carry

    lax.fori_loop(0, subs // GROUP, grid_group, 0)
    for sub in range(subs):
        half_ref[sub * SUB : (sub + 1) * SUB, :] = jnp.dot(
            right_ref[:SUB, :], stack_ref[sub], preferred_element_type=jnp.float32
        ).astype(jnp.bfloat16)

    for group in range(subs // GROUP):
        base = group * GROUP
        patches = jnp.dot(
            half_ref[base * SUB : (base + GROUP) * SUB, :],
            right_ref[...],
            preferred_element_type=jnp.float32,
        )
        for member in range(GROUP):
            pad_ref[member, SUB : 2 * SUB, :] = patches[member * SUB : (member + 1) * SUB]
        for member in range(GROUP):
            sub = base + member
            facet, slot = next_slot(facet_ref, used_ref, sub)
            row = row_ref[sub]
            placed = pad_ref[member, pl.ds(SUB - row, F_ROWS), :].astype(jnp.bfloat16)
            send_ref[pl.ds(facet * chans, chans), slot] = placed.reshape(chans, shard, LANES)
            where_ref[(facet ^ me) * cap + slot] = VALID_BIT + row * FACET + col_ref[sub]
    for number, meta_ref in enumerate(meta_refs):
        for slot in range(cap):
            meta_ref[slot] = where_ref[number * cap + slot]


def pick_kernel(facets, cap, *refs):
    meta_ref, model_ref, columns_in, rows_in, *refs = refs
    back_out, refs = refs[:facets], refs[facets:]
    columns_ref, rows_ref, back_ref, list_ref, sems, out_sems, *wide_refs = refs
    slots = facets * cap
    fetch([(columns_in, columns_ref), (rows_in, rows_ref)], sems)
    found = 0
    for source in range(facets):
        values = [meta_ref[source * cap + slot] for slot in range(cap)]
        for slot, packed in enumerate(values):
            list_ref[found] = (packed & (VALID_BIT - 1)) * slots + source * cap + slot
            found = found + (packed >= VALID_BIT).astype(jnp.int32)
    low_lanes = lax.broadcasted_iota(jnp.int32, (SUB, LANES), 1) < SUB

    def columns_of(position, wide_ref):
        entry = list_ref[position]
        where = lax.div(entry, slots)
        col = where & (FACET - 1)
        block = jnp.minimum(lax.div(col, LANES), FACET // LANES - 2)
        slab = model_ref[:, pl.ds(pl.multiple_of(block * LANES, LANES), 2 * LANES)]
        table = columns_ref[pl.ds(SPAN - col + block * LANES, 2 * LANES), :]
        wide_ref[...] = jnp.dot(
            slab, table.astype(jnp.bfloat16), preferred_element_type=jnp.float32
        )
        return lax.rem(entry, slots), lax.div(where, FACET)

    def rows_of(row, wide_ref):
        half = wide_ref[pl.ds(2 * row, 2 * SUB), :].astype(jnp.bfloat16)
        return jnp.dot(rows_ref[...], half, preferred_element_type=jnp.float32)

    def finish(image):
        turned = pltpu.roll(image[SUB:], SUB, 1)
        return (image[:SUB] + jnp.where(low_lanes, -turned, turned)).astype(jnp.bfloat16)

    def one_group(group, carry):
        places = [
            columns_of(jnp.minimum(group * PICK_GROUP + member, found - 1), wide_refs[member])
            for member in range(PICK_GROUP)
        ]
        images = [rows_of(row, wide_refs[member]) for member, (_, row) in enumerate(places)]
        images = [finish(image) for image in images]
        for (index, _), image in zip(places, images):
            back_ref[index] = image
        return carry

    lax.fori_loop(0, lax.div(found + PICK_GROUP - 1, PICK_GROUP), one_group, 0)
    fetch(
        [
            (back_ref.at[pl.ds(number * cap, cap)], back_out[number])
            for number in range(facets)
        ],
        out_sems,
    )


def add_kernel(facets, chans, cap, meta_ref, recv_ref, image_ref, *canvas_refs):
    shard = F_ROWS // chans
    facet, chan = lax.axis_index("facet"), lax.axis_index("chan")
    for canvas_ref in canvas_refs:
        canvas_ref[...] = jnp.zeros_like(canvas_ref)
    lanes = lax.broadcasted_iota(jnp.int32, (shard, LANES), 1)
    within = lanes & (SUB - 1)

    def load(packed, index):
        col = jnp.where(packed >= VALID_BIT, packed & (FACET - 1), FACET + SUB)
        shift = col & (SUB - 1)
        values = recv_ref[index].astype(jnp.float32)
        near = jnp.where(within >= shift, pltpu.roll(values, shift, 1), 0.0)
        far = jnp.where(within >= shift, 0.0, pltpu.roll(values, shift + SUB, 1))
        return lax.div(col, SUB) * LANES, near, far

    def one_source(source, carry):
        source_facet = (source & (facets - 1)) ^ facet
        source_chan = lax.div(source, facets) ^ chan
        first = (source_facet * chans + source_chan) * cap
        packs = [meta_ref[source * cap + slot] for slot in range(cap)]
        loaded = [load(packed, first + slot) for slot, packed in enumerate(packs)]
        for slot, (start, near, far) in enumerate(loaded):
            canvas_ref = canvas_refs[slot % CANVASES]
            canvas_ref[:, pl.ds(pl.multiple_of(start, LANES), LANES)] += near
            canvas_ref[:, pl.ds(pl.multiple_of(start + LANES, LANES), LANES)] += far
        return carry

    lax.fori_loop(0, facets * chans, one_source, 0, unroll=4)
    for block in range(FACET // LANES):
        first, second = [
            sum(ref[:, (2 * block + half) * LANES : (2 * block + half + 1) * LANES] for ref in canvas_refs)
            for half in range(2)
        ]
        place = slice(block * LANES, (block + 1) * LANES)
        image_ref[:, 0, place] = jnp.where(lanes < SUB, first, pltpu.roll(second, SUB, 1))
        image_ref[:, 1, place] = jnp.where(lanes < SUB, pltpu.roll(first, SUB, 1), second)


def degrid_kernel(facets, facet_in, count_in, vis_in, coord_in, *refs):
    back_in, refs = refs[:facets], refs[facets:]
    out_ref, facet_ref, count_ref, vis_ref, coord_ref, back_ref, used_ref, sems = refs
    subs = vis_ref.shape[0]
    fetch(
        [
            (facet_in, facet_ref),
            (count_in, count_ref),
            (vis_in, vis_ref),
            (coord_in, coord_ref),
        ]
        + [(back_in[number], back_ref.at[number]) for number in range(facets)],
        sems,
    )
    me = lax.axis_index("facet")
    clear_used(used_ref, facets)
    low_lanes = lax.broadcasted_iota(jnp.int32, (SUB, LANES), 1) < SUB

    def one_group(group, carry):
        for member in range(GROUP):
            sub = group * GROUP + member
            facet, slot = next_slot(facet_ref, used_ref, sub)
            kernel_u = gaussian(coord_ref[sub, 0:1, :]).astype(jnp.bfloat16).astype(jnp.float32)
            kernel_v = gaussian(coord_ref[sub, 1:2, :]).astype(jnp.bfloat16)
            grid = back_ref[facet ^ me, slot].astype(jnp.float32)
            split = jnp.concatenate(
                [jnp.where(low_lanes, grid, 0.0), jnp.where(low_lanes, 0.0, grid)], 0
            ).astype(jnp.bfloat16)
            lines = jnp.dot(
                split,
                jnp.concatenate([kernel_v, kernel_v], 0),
                preferred_element_type=jnp.float32,
            )
            live = live_row(count_ref[sub])
            for part in range(2):
                predicted = jnp.sum(
                    lines[part * SUB : (part + 1) * SUB] * kernel_u, 0, keepdims=True
                )
                seen = vis_ref[sub, part : part + 1, :]
                out_ref[sub, part : part + 1, :] = jnp.where(live, seen - predicted, 0.0)
        return carry

    lax.fori_loop(0, subs // GROUP, one_group, 0)


def smem():
    return pl.BlockSpec(memory_space=pltpu.SMEM)


def vmem():
    return pl.BlockSpec(memory_space=pltpu.VMEM)


def hbm():
    return pl.BlockSpec(memory_space=pltpu.HBM)


def params():
    return pltpu.CompilerParams(vmem_limit_bytes=VMEM_LIMIT)


def copy_sems(count):
    return pltpu.SemaphoreType.DMA((count,))


def in_hbm(values):
    return pltpu.with_memory_space_constraint(values, pltpu.HBM)


def partner(values, axis, bit):
    return lax.ppermute(
        values, axis, [(index, index ^ bit) for index in range(lax.axis_size(axis))]
    )


def per_device(
    visibility, uv_coords, vis_count, subgrid_facet, row_offset, col_offset, model_facet
):
    facets = lax.axis_size("facet")
    chans = lax.axis_size("chan")
    subs = visibility.shape[0]
    cap = max(2, 2 * subs // facets)
    shard = F_ROWS // chans
    slots = facets * cap
    total = slots * chans
    facet_ids = subgrid_facet[:, 0]

    grid_inputs = (
        facet_ids, row_offset, col_offset, vis_count, visibility, uv_coords, forward_table()
    )
    send, *metas = pl.pallas_call(
        functools.partial(grid_kernel, facets, chans),
        out_shape=tuple(
            [jax.ShapeDtypeStruct((facets * chans, cap, shard, LANES), jnp.bfloat16)]
            + [jax.ShapeDtypeStruct((WORDS,), jnp.int32)] * facets
        ),
        in_specs=[hbm()] * 7,
        out_specs=tuple([vmem()] + [smem()] * facets),
        scratch_shapes=[
            pltpu.SMEM((subs,), jnp.int32),
            pltpu.SMEM((subs,), jnp.int32),
            pltpu.SMEM((subs,), jnp.int32),
            pltpu.SMEM((subs,), jnp.int32),
            pltpu.VMEM((subs, 2, NV), jnp.float32),
            pltpu.VMEM((subs, 2, NV), jnp.float32),
            pltpu.VMEM((LANES, LANES), jnp.bfloat16),
            pltpu.VMEM((subs, LANES, LANES), jnp.bfloat16),
            pltpu.VMEM((subs * SUB, LANES), jnp.bfloat16),
            pltpu.VMEM((GROUP, 3 * SUB, LANES), jnp.float32),
            pltpu.SMEM((facets,), jnp.int32),
            pltpu.SMEM((slots,), jnp.int32),
            copy_sems(7),
        ],
        compiler_params=params(),
        name="grid",
    )(*[in_hbm(value) for value in grid_inputs])
    metas = metas[:1] + [partner(metas[bit], "facet", bit) for bit in range(1, facets)]
    mine = jnp.concatenate([values[:cap] for values in metas])
    every = mine
    bit = 1
    while 2 * bit < chans:
        every = jnp.concatenate([every, partner(every, "chan", bit)])
        bit *= 2
    rest = partner(every, "chan", bit)

    send, model_facet = lax.optimization_barrier((send, model_facet))
    recv = lax.all_to_all(send, ("facet", "chan"), split_axis=0, concat_axis=0, tiled=True)

    columns, rows = inverse_tables()
    model = model_facet.reshape(2 * F_ROWS, FACET)
    back = pl.pallas_call(
        functools.partial(pick_kernel, facets, cap),
        out_shape=tuple([jax.ShapeDtypeStruct((cap, SUB, LANES), jnp.bfloat16)] * facets),
        in_specs=[smem(), vmem(), hbm(), hbm()],
        out_specs=tuple([hbm()] * facets),
        scratch_shapes=[
            pltpu.VMEM((2 * SPAN + SUB, LANES), jnp.float32),
            pltpu.VMEM((2 * SUB, 2 * SUB), jnp.bfloat16),
            pltpu.VMEM((slots, SUB, LANES), jnp.bfloat16),
            pltpu.SMEM((slots + 1,), jnp.int32),
            copy_sems(2),
            copy_sems(facets),
        ]
        + [pltpu.VMEM((2 * F_ROWS, LANES), jnp.float32)] * PICK_GROUP,
        compiler_params=params(),
        name="pick",
    )(mine, model, in_hbm(columns), in_hbm(rows))
    returned = [back[0]] + [partner(back[bit], "facet", bit) for bit in range(1, facets)]

    residual_vis = pl.pallas_call(
        functools.partial(degrid_kernel, facets),
        out_shape=jax.ShapeDtypeStruct((subs, 2, NV), jnp.float32),
        in_specs=[hbm()] * (4 + facets),
        out_specs=vmem(),
        scratch_shapes=[
            pltpu.SMEM((subs,), jnp.int32),
            pltpu.SMEM((subs,), jnp.int32),
            pltpu.VMEM((subs, 2, NV), jnp.float32),
            pltpu.VMEM((subs, 2, NV), jnp.float32),
            pltpu.VMEM((facets, cap, SUB, LANES), jnp.bfloat16),
            pltpu.SMEM((facets,), jnp.int32),
            copy_sems(4 + facets),
        ],
        compiler_params=params(),
        name="degrid",
    )(*[in_hbm(value) for value in (facet_ids, vis_count, visibility, uv_coords)], *returned)

    every, rest, residual_vis = lax.optimization_barrier((every, rest, residual_vis))
    facet_image = pl.pallas_call(
        functools.partial(add_kernel, facets, chans, cap),
        out_shape=jax.ShapeDtypeStruct((shard, 2, FACET), jnp.float32),
        in_specs=[smem(), vmem()],
        out_specs=vmem(),
        scratch_shapes=[pltpu.VMEM((shard, 2 * FACET + 3 * LANES), jnp.float32)] * CANVASES,
        compiler_params=params(),
        name="add",
    )(jnp.concatenate([every, rest]), recv.reshape(total, shard, LANES))
    return (facet_image[None], residual_vis)


def solution(mesh):
    in_specs = (
        P(("facet", "chan"), None, None),
        P(("facet", "chan"), None, None),
        P(("facet", "chan")),
        P(("facet", "chan"), None),
        P(("facet", "chan")),
        P(("facet", "chan")),
        P("facet", None, None, None),
    )
    out_specs = (P("facet", "chan", None, None), P(("facet", "chan"), None, None))
    return jax.shard_map(
        per_device, mesh=mesh, in_specs=in_specs, out_specs=out_specs, check_vma=False
    )
```

```python
import functools
import math

import jax
import jax.numpy as jnp
import numpy as np
from jax import lax
from jax.experimental import pallas as pl
from jax.experimental.pallas import tpu as pltpu
from jax.sharding import PartitionSpec as P

SUB = 64
FACET = 4096
F_ROWS = 128
NV = 512
LANES = 128
VALID_BIT = 1 << 20
GROUP = 4
WORDS = 128

SPAN = 3 * SUB
PICK_GROUP = 8
CANVASES = 2

VMEM_LIMIT = 48 * 1024 * 1024


def dft_arrays():
    index_line = np.arange(SUB)
    phase = (index_line[:, None] * index_line[None, :]) % SUB
    angle = (2.0 * math.pi * phase / SUB).astype(np.float32)
    cos_table = np.cos(angle) / np.float32(math.sqrt(SUB))
    sin_table = -np.sin(angle) / np.float32(math.sqrt(SUB))
    return cos_table.astype(np.float32), sin_table.astype(np.float32)


def forward_table():
    cos_table, sin_table = dft_arrays()
    right = np.concatenate(
        [np.concatenate([cos_table, sin_table], 1), np.concatenate([-sin_table, cos_table], 1)], 0
    )
    return jnp.asarray(right, jnp.bfloat16)


def inverse_tables():
    cos_table, sin_table = dft_arrays()
    sin_table = -sin_table
    columns = np.zeros((2 * SPAN + SUB, LANES), np.float32)
    columns[SPAN : SPAN + SUB] = np.concatenate([cos_table, sin_table], 1)
    rows = np.zeros((2 * SUB, 2 * SUB), np.float32)
    rows[:SUB, 0::2] = cos_table
    rows[:SUB, 1::2] = -sin_table
    rows[SUB:, 0::2] = sin_table
    rows[SUB:, 1::2] = cos_table
    columns = columns.astype(jnp.bfloat16).astype(np.float32)
    return jnp.asarray(columns), jnp.asarray(rows, jnp.bfloat16)


def gaussian(coord_row):
    pixel = lax.broadcasted_iota(jnp.int32, (SUB, NV), 0).astype(jnp.float32)
    delta = pixel - coord_row
    return jnp.exp(-(delta * delta))


def live_row(count):
    return lax.broadcasted_iota(jnp.int32, (1, NV), 1) < count


def start(copies, sems):
    started = [
        pltpu.make_async_copy(source, target, sems.at[number])
        for number, (source, target) in enumerate(copies)
    ]
    for copy in started:
        copy.start()
    return started


def fetch(copies, sems):
    for copy in start(copies, sems):
        copy.wait()


def next_slot(facet_ref, used_ref, sub):
    facet = facet_ref[sub]
    slot = used_ref[facet]
    used_ref[facet] = slot + 1
    return facet, slot


def clear_used(used_ref, facets):
    for facet in range(facets):
        used_ref[facet] = 0


def grid_kernel(
    facets, chans, facet_in, row_in, col_in, count_in, vis_in, coord_in, right_in, send_ref, *refs
):
    meta_refs, refs = refs[:facets], refs[facets:]
    facet_ref, row_ref, col_ref, count_ref, vis_ref, coord_ref, right_ref, *refs = refs
    stack_ref, half_ref, pad_ref, used_ref, where_ref, sems = refs
    me = lax.axis_index("facet")
    cap = send_ref.shape[1]
    subs = vis_ref.shape[0]
    shard = F_ROWS // chans
    fetch(
        [
            (facet_in, facet_ref),
            (row_in, row_ref),
            (col_in, col_ref),
            (count_in, count_ref),
            (vis_in, vis_ref),
            (coord_in, coord_ref),
            (right_in, right_ref),
        ],
        sems,
    )
    clear_used(used_ref, facets)
    for index in range(facets * cap):
        where_ref[index] = 0
    for member in range(GROUP):
        pad_ref[member, :SUB, :] = jnp.zeros((SUB, LANES), jnp.float32)
        pad_ref[member, 2 * SUB :, :] = jnp.zeros((SUB, LANES), jnp.float32)
    low_lanes = lax.broadcasted_iota(jnp.int32, (SUB, LANES), 1) < SUB

    def grid_one(sub):
        kernel_u = gaussian(coord_ref[sub, 0:1, :]).astype(jnp.bfloat16)
        kernel_v = gaussian(coord_ref[sub, 1:2, :])
        live = live_row(count_ref[sub])
        spread = jnp.concatenate(
            [
                (jnp.where(live, vis_ref[sub, part : part + 1, :], 0.0) * kernel_v).astype(
                    jnp.bfloat16
                )
                for part in range(2)
            ],
            0,
        )
        gridded = lax.dot_general(
            kernel_u, spread, (((1,), (1,)), ((), ())), preferred_element_type=jnp.float32
        )
        swapped = pltpu.roll(gridded, SUB, 1)
        swapped = jnp.where(low_lanes, -swapped, swapped)
        stack_ref[sub] = jnp.concatenate([gridded, swapped], 0).astype(jnp.bfloat16)

    def grid_group(group, carry):
        for member in range(GROUP):
            grid_one(group * GROUP + member)
        return carry

    lax.fori_loop(0, subs // GROUP, grid_group, 0, unroll=True)
    for sub in range(subs):
        half_ref[sub * SUB : (sub + 1) * SUB, :] = jnp.dot(
            right_ref[:SUB, :], stack_ref[sub], preferred_element_type=jnp.float32
        ).astype(jnp.bfloat16)

    for group in range(subs // GROUP):
        base = group * GROUP
        patches = jnp.dot(
            half_ref[base * SUB : (base + GROUP) * SUB, :],
            right_ref[...],
            preferred_element_type=jnp.float32,
        )
        for member in range(GROUP):
            pad_ref[member, SUB : 2 * SUB, :] = patches[member * SUB : (member + 1) * SUB]
        for member in range(GROUP):
            sub = base + member
            facet, slot = next_slot(facet_ref, used_ref, sub)
            row = row_ref[sub]
            placed = pad_ref[member, pl.ds(SUB - row, F_ROWS), :].astype(jnp.bfloat16)
            send_ref[pl.ds(facet * chans, chans), slot] = placed.reshape(chans, shard, LANES)
            where_ref[(facet ^ me) * cap + slot] = VALID_BIT + row * FACET + col_ref[sub]
    for number, meta_ref in enumerate(meta_refs):
        for slot in range(cap):
            meta_ref[slot] = where_ref[number * cap + slot]


def pick_kernel(facets, cap, *refs):
    meta_ref, model_ref, columns_in, rows_in, *refs = refs
    back_out, refs = refs[:facets], refs[facets:]
    columns_ref, rows_ref, back_ref, list_ref, sems, out_sems, *wide_refs = refs
    slots = facets * cap
    fetch([(columns_in, columns_ref), (rows_in, rows_ref)], sems)
    found = 0
    for source in range(facets):
        values = [meta_ref[source * cap + slot] for slot in range(cap)]
        for slot, packed in enumerate(values):
            list_ref[found] = (packed & (VALID_BIT - 1)) * slots + source * cap + slot
            found = found + (packed >= VALID_BIT).astype(jnp.int32)
    low_lanes = lax.broadcasted_iota(jnp.int32, (SUB, LANES), 1) < SUB

    def columns_of(position, wide_ref):
        entry = list_ref[position]
        where = lax.div(entry, slots)
        col = where & (FACET - 1)
        block = jnp.minimum(lax.div(col, LANES), FACET // LANES - 2)
        slab = model_ref[:, pl.ds(pl.multiple_of(block * LANES, LANES), 2 * LANES)]
        table = columns_ref[pl.ds(SPAN - col + block * LANES, 2 * LANES), :]
        wide_ref[...] = jnp.dot(
            slab, table.astype(jnp.bfloat16), preferred_element_type=jnp.float32
        )
        return lax.rem(entry, slots), lax.div(where, FACET)

    def rows_of(row, wide_ref):
        half = wide_ref[pl.ds(2 * row, 2 * SUB), :].astype(jnp.bfloat16)
        return jnp.dot(rows_ref[...], half, preferred_element_type=jnp.float32)

    def finish(image):
        turned = pltpu.roll(image[SUB:], SUB, 1)
        return (image[:SUB] + jnp.where(low_lanes, -turned, turned)).astype(jnp.bfloat16)

    def one_group(group, carry):
        places = [
            columns_of(jnp.minimum(group * PICK_GROUP + member, found - 1), wide_refs[member])
            for member in range(PICK_GROUP)
        ]
        images = [rows_of(row, wide_refs[member]) for member, (_, row) in enumerate(places)]
        images = [finish(image) for image in images]
        for (index, _), image in zip(places, images):
            back_ref[index] = image
        return carry

    lax.fori_loop(0, lax.div(found + PICK_GROUP - 1, PICK_GROUP), one_group, 0)
    fetch(
        [
            (back_ref.at[pl.ds(number * cap, cap)], back_out[number])
            for number in range(facets)
        ],
        out_sems,
    )


def add_kernel(
    facets, chans, cap, meta_in, recv_in, image_ref, meta_ref, recv_ref, sems, *canvas_refs
):
    shard = F_ROWS // chans
    facet, chan = lax.axis_index("facet"), lax.axis_index("chan")
    group = chans * cap
    groups = [pl.ds((number ^ facet) * group, group) for number in range(facets)]
    loads = start(
        [(meta_in, meta_ref)] + [(recv_in.at[part], recv_ref.at[part]) for part in groups], sems
    )
    for canvas_ref in canvas_refs:
        canvas_ref[...] = jnp.zeros_like(canvas_ref)
    loads[0].wait()
    lanes = lax.broadcasted_iota(jnp.int32, (shard, LANES), 1)
    within = lanes & (SUB - 1)

    def load(packed, index):
        col = jnp.where(packed >= VALID_BIT, packed & (FACET - 1), FACET + SUB)
        shift = col & (SUB - 1)
        values = recv_ref[index].astype(jnp.float32)
        turned = pltpu.roll(values, col & (LANES - 1), 1)
        near = jnp.where(within >= shift, turned, 0.0)
        return lax.div(col, SUB) * LANES, near, jnp.where(within >= shift, 0.0, turned)

    def one_source(number, source, carry):
        first = ((number ^ facet) * chans + (source ^ chan)) * cap
        place = (source * facets + number) * cap
        packs = [meta_ref[place + slot] for slot in range(cap)]
        loaded = [load(packed, first + slot) for slot, packed in enumerate(packs)]
        for slot, (start, near, far) in enumerate(loaded):
            canvas_ref = canvas_refs[slot % CANVASES]
            place = pl.ds(pl.multiple_of(start, LANES), 2 * LANES)
            canvas_ref[:, place] += jnp.concatenate([near, far], 1)
        return carry

    for number in range(facets):
        loads[1 + number].wait()
        lax.fori_loop(0, chans, functools.partial(one_source, number), 0, unroll=8)
    for block in range(FACET // LANES):
        first, second = [
            sum(ref[:, (2 * block + half) * LANES : (2 * block + half + 1) * LANES] for ref in canvas_refs)
            for half in range(2)
        ]
        place = slice(block * LANES, (block + 1) * LANES)
        image_ref[:, 0, place] = jnp.where(lanes < SUB, first, second)
        image_ref[:, 1, place] = pltpu.roll(jnp.where(lanes < SUB, second, first), SUB, 1)


def degrid_kernel(facets, facet_in, count_in, vis_in, coord_in, *refs):
    back_in, refs = refs[:facets], refs[facets:]
    out_ref, facet_ref, count_ref, vis_ref, coord_ref, back_ref, used_ref, sems = refs
    subs = vis_ref.shape[0]
    fetch(
        [
            (facet_in, facet_ref),
            (count_in, count_ref),
            (vis_in, vis_ref),
            (coord_in, coord_ref),
        ]
        + [(back_in[number], back_ref.at[number]) for number in range(facets)],
        sems,
    )
    me = lax.axis_index("facet")
    clear_used(used_ref, facets)
    low_lanes = lax.broadcasted_iota(jnp.int32, (SUB, LANES), 1) < SUB

    def one_group(group, carry):
        for member in range(GROUP):
            sub = group * GROUP + member
            facet, slot = next_slot(facet_ref, used_ref, sub)
            kernel_u = gaussian(coord_ref[sub, 0:1, :]).astype(jnp.bfloat16).astype(jnp.float32)
            kernel_v = gaussian(coord_ref[sub, 1:2, :]).astype(jnp.bfloat16)
            grid = back_ref[facet ^ me, slot].astype(jnp.float32)
            split = jnp.concatenate(
                [jnp.where(low_lanes, grid, 0.0), jnp.where(low_lanes, 0.0, grid)], 0
            ).astype(jnp.bfloat16)
            lines = jnp.dot(
                split,
                jnp.concatenate([kernel_v, kernel_v], 0),
                preferred_element_type=jnp.float32,
            )
            live = live_row(count_ref[sub])
            for part in range(2):
                predicted = jnp.sum(
                    lines[part * SUB : (part + 1) * SUB] * kernel_u, 0, keepdims=True
                )
                seen = vis_ref[sub, part : part + 1, :]
                out_ref[sub, part : part + 1, :] = jnp.where(live, seen - predicted, 0.0)
        return carry

    lax.fori_loop(0, subs // GROUP, one_group, 0)


def smem():
    return pl.BlockSpec(memory_space=pltpu.SMEM)


def vmem():
    return pl.BlockSpec(memory_space=pltpu.VMEM)


def hbm():
    return pl.BlockSpec(memory_space=pltpu.HBM)


def params():
    return pltpu.CompilerParams(vmem_limit_bytes=VMEM_LIMIT)


def copy_sems(count):
    return pltpu.SemaphoreType.DMA((count,))


def in_hbm(values):
    return pltpu.with_memory_space_constraint(values, pltpu.HBM)


def partner(values, axis, bit):
    return lax.ppermute(
        values, axis, [(index, index ^ bit) for index in range(lax.axis_size(axis))]
    )


def per_device(
    visibility, uv_coords, vis_count, subgrid_facet, row_offset, col_offset, model_facet
):
    facets = lax.axis_size("facet")
    chans = lax.axis_size("chan")
    subs = visibility.shape[0]
    cap = max(2, 2 * subs // facets)
    shard = F_ROWS // chans
    slots = facets * cap
    total = slots * chans
    facet_ids = subgrid_facet[:, 0]

    grid_inputs = (
        facet_ids, row_offset, col_offset, vis_count, visibility, uv_coords, forward_table()
    )
    send, *metas = pl.pallas_call(
        functools.partial(grid_kernel, facets, chans),
        out_shape=tuple(
            [jax.ShapeDtypeStruct((facets * chans, cap, shard, LANES), jnp.bfloat16)]
            + [jax.ShapeDtypeStruct((WORDS,), jnp.int32)] * facets
        ),
        in_specs=[hbm()] * 7,
        out_specs=tuple([vmem()] + [smem()] * facets),
        scratch_shapes=[
            pltpu.SMEM((subs,), jnp.int32),
            pltpu.SMEM((subs,), jnp.int32),
            pltpu.SMEM((subs,), jnp.int32),
            pltpu.SMEM((subs,), jnp.int32),
            pltpu.VMEM((subs, 2, NV), jnp.float32),
            pltpu.VMEM((subs, 2, NV), jnp.float32),
            pltpu.VMEM((LANES, LANES), jnp.bfloat16),
            pltpu.VMEM((subs, LANES, LANES), jnp.bfloat16),
            pltpu.VMEM((subs * SUB, LANES), jnp.bfloat16),
            pltpu.VMEM((GROUP, 3 * SUB, LANES), jnp.float32),
            pltpu.SMEM((facets,), jnp.int32),
            pltpu.SMEM((slots,), jnp.int32),
            copy_sems(7),
        ],
        compiler_params=params(),
        name="grid",
    )(*[in_hbm(value) for value in grid_inputs])
    metas = metas[:1] + [partner(metas[bit], "facet", bit) for bit in range(1, facets)]
    mine = jnp.concatenate([values[:cap] for values in metas])
    every = mine
    bit = 1
    while 2 * bit < chans:
        every = jnp.concatenate([every, partner(every, "chan", bit)])
        bit *= 2
    rest = partner(every, "chan", bit)

    send, model_facet = lax.optimization_barrier((send, model_facet))
    recv = lax.all_to_all(send, ("facet", "chan"), split_axis=0, concat_axis=0, tiled=True)

    columns, rows = inverse_tables()
    model = model_facet.reshape(2 * F_ROWS, FACET)
    back = pl.pallas_call(
        functools.partial(pick_kernel, facets, cap),
        out_shape=tuple([jax.ShapeDtypeStruct((cap, SUB, LANES), jnp.bfloat16)] * facets),
        in_specs=[smem(), vmem(), hbm(), hbm()],
        out_specs=tuple([hbm()] * facets),
        scratch_shapes=[
            pltpu.VMEM((2 * SPAN + SUB, LANES), jnp.float32),
            pltpu.VMEM((2 * SUB, 2 * SUB), jnp.bfloat16),
            pltpu.VMEM((slots, SUB, LANES), jnp.bfloat16),
            pltpu.SMEM((slots + 1,), jnp.int32),
            copy_sems(2),
            copy_sems(facets),
        ]
        + [pltpu.VMEM((2 * F_ROWS, LANES), jnp.float32)] * PICK_GROUP,
        compiler_params=params(),
        name="pick",
    )(mine, model, in_hbm(columns), in_hbm(rows))
    returned = [back[0]] + [partner(back[bit], "facet", bit) for bit in range(1, facets)]

    residual_vis = pl.pallas_call(
        functools.partial(degrid_kernel, facets),
        out_shape=jax.ShapeDtypeStruct((subs, 2, NV), jnp.float32),
        in_specs=[hbm()] * (4 + facets),
        out_specs=vmem(),
        scratch_shapes=[
            pltpu.SMEM((subs,), jnp.int32),
            pltpu.SMEM((subs,), jnp.int32),
            pltpu.VMEM((subs, 2, NV), jnp.float32),
            pltpu.VMEM((subs, 2, NV), jnp.float32),
            pltpu.VMEM((facets, cap, SUB, LANES), jnp.bfloat16),
            pltpu.SMEM((facets,), jnp.int32),
            copy_sems(4 + facets),
        ],
        compiler_params=params(),
        name="degrid",
    )(*[in_hbm(value) for value in (facet_ids, vis_count, visibility, uv_coords)], *returned)

    every, rest, residual_vis = lax.optimization_barrier((every, rest, residual_vis))
    facet_image = pl.pallas_call(
        functools.partial(add_kernel, facets, chans, cap),
        out_shape=jax.ShapeDtypeStruct((shard, 2, FACET), jnp.float32),
        in_specs=[hbm(), hbm()],
        out_specs=vmem(),
        scratch_shapes=[
            pltpu.SMEM((total,), jnp.int32),
            pltpu.VMEM((total, shard, LANES), jnp.bfloat16),
            copy_sems(1 + facets),
        ]
        + [pltpu.VMEM((shard, 2 * FACET + 3 * LANES), jnp.float32)] * CANVASES,
        compiler_params=params(),
        name="add",
    )(jnp.concatenate([every, rest]), recv.reshape(total, shard, LANES))
    return (facet_image[None], residual_vis)


def solution(mesh):
    in_specs = (
        P(("facet", "chan"), None, None),
        P(("facet", "chan"), None, None),
        P(("facet", "chan")),
        P(("facet", "chan"), None),
        P(("facet", "chan")),
        P(("facet", "chan")),
        P("facet", None, None, None),
    )
    out_specs = (P("facet", "chan", None, None), P(("facet", "chan"), None, None))
    return jax.shard_map(
        per_device, mesh=mesh, in_specs=in_specs, out_specs=out_specs, check_vma=False
    )
```

```python
import functools
import math

import jax
import jax.numpy as jnp
import numpy as np
from jax import lax
from jax.experimental import pallas as pl
from jax.experimental.pallas import tpu as pltpu
from jax.sharding import PartitionSpec as P

SUB = 64
FACET = 4096
F_ROWS = 128
NV = 512
LANES = 128
VALID_BIT = 1 << 20
GROUP = 4
WORDS = 128

SPAN = 3 * SUB
PICK_GROUP = 16
CANVASES = 2
PARTS = 4

VMEM_LIMIT = 48 * 1024 * 1024


def dft_arrays():
    index_line = np.arange(SUB)
    phase = (index_line[:, None] * index_line[None, :]) % SUB
    angle = (2.0 * math.pi * phase / SUB).astype(np.float32)
    cos_table = np.cos(angle) / np.float32(math.sqrt(SUB))
    sin_table = -np.sin(angle) / np.float32(math.sqrt(SUB))
    return cos_table.astype(np.float32), sin_table.astype(np.float32)


def forward_table():
    cos_table, sin_table = dft_arrays()
    right = np.concatenate(
        [np.concatenate([cos_table, sin_table], 1), np.concatenate([-sin_table, cos_table], 1)], 0
    )
    return jnp.asarray(right, jnp.bfloat16)


def inverse_tables():
    cos_table, sin_table = dft_arrays()
    sin_table = -sin_table
    columns = np.zeros((2 * SPAN + SUB, LANES), np.float32)
    columns[SPAN : SPAN + SUB] = np.concatenate([cos_table, sin_table], 1)
    rows = np.zeros((2 * SUB, 2 * SUB), np.float32)
    rows[:SUB, 0::2] = cos_table
    rows[:SUB, 1::2] = -sin_table
    rows[SUB:, 0::2] = sin_table
    rows[SUB:, 1::2] = cos_table
    columns = columns.astype(jnp.bfloat16).astype(np.float32)
    return jnp.asarray(columns), jnp.asarray(rows, jnp.bfloat16)


def gaussian(coord_row):
    pixel = lax.broadcasted_iota(jnp.int32, (SUB, NV), 0).astype(jnp.float32)
    delta = pixel - coord_row
    return jnp.exp(-(delta * delta))


def live_row(count):
    return lax.broadcasted_iota(jnp.int32, (1, NV), 1) < count


def start(copies, sems):
    started = [
        pltpu.make_async_copy(source, target, sems.at[number])
        for number, (source, target) in enumerate(copies)
    ]
    for copy in started:
        copy.start()
    return started


def fetch(copies, sems):
    for copy in start(copies, sems):
        copy.wait()


def next_slot(facet_ref, used_ref, sub):
    facet = facet_ref[sub]
    slot = used_ref[facet]
    used_ref[facet] = slot + 1
    return facet, slot


def clear_used(used_ref, facets):
    for facet in range(facets):
        used_ref[facet] = 0


def grid_kernel(
    facets, chans, facet_in, row_in, col_in, count_in, vis_in, coord_in, right_in, send_ref, *refs
):
    meta_refs, refs = refs[:facets], refs[facets:]
    facet_ref, row_ref, col_ref, count_ref, vis_ref, coord_ref, right_ref, *refs = refs
    stack_ref, half_ref, pad_ref, used_ref, where_ref, sems = refs
    me = lax.axis_index("facet")
    cap = send_ref.shape[2]
    subs = vis_ref.shape[0]
    shard = F_ROWS // chans
    fetch(
        [
            (facet_in, facet_ref),
            (row_in, row_ref),
            (col_in, col_ref),
            (count_in, count_ref),
            (vis_in, vis_ref),
            (coord_in, coord_ref),
            (right_in, right_ref),
        ],
        sems,
    )
    clear_used(used_ref, facets)
    for index in range(facets * cap):
        where_ref[index] = 0
    for member in range(GROUP):
        pad_ref[member, :SUB, :] = jnp.zeros((SUB, LANES), jnp.float32)
        pad_ref[member, 2 * SUB :, :] = jnp.zeros((SUB, LANES), jnp.float32)
    low_lanes = lax.broadcasted_iota(jnp.int32, (SUB, LANES), 1) < SUB

    def grid_one(sub):
        kernel_u = gaussian(coord_ref[sub, 0:1, :]).astype(jnp.bfloat16)
        kernel_v = gaussian(coord_ref[sub, 1:2, :])
        live = live_row(count_ref[sub])
        spread = jnp.concatenate(
            [
                (jnp.where(live, vis_ref[sub, part : part + 1, :], 0.0) * kernel_v).astype(
                    jnp.bfloat16
                )
                for part in range(2)
            ],
            0,
        )
        gridded = lax.dot_general(
            kernel_u, spread, (((1,), (1,)), ((), ())), preferred_element_type=jnp.float32
        )
        swapped = pltpu.roll(gridded, SUB, 1)
        swapped = jnp.where(low_lanes, -swapped, swapped)
        stack_ref[sub] = jnp.concatenate([gridded, swapped], 0).astype(jnp.bfloat16)

    def grid_group(group, carry):
        for member in range(GROUP):
            grid_one(group * GROUP + member)
        return carry

    lax.fori_loop(0, subs // GROUP, grid_group, 0, unroll=True)
    for sub in range(subs):
        half_ref[sub * SUB : (sub + 1) * SUB, :] = jnp.dot(
            right_ref[:SUB, :], stack_ref[sub], preferred_element_type=jnp.float32
        ).astype(jnp.bfloat16)

    for group in range(subs // GROUP):
        base = group * GROUP
        patches = jnp.dot(
            half_ref[base * SUB : (base + GROUP) * SUB, :],
            right_ref[...],
            preferred_element_type=jnp.float32,
        )
        for member in range(GROUP):
            patch = patches[member * SUB : (member + 1) * SUB]
            turned = pltpu.roll(patch, col_ref[base + member] & (LANES - 1), 1)
            pad_ref[member, SUB : 2 * SUB, :] = turned
        for member in range(GROUP):
            sub = base + member
            facet, slot = next_slot(facet_ref, used_ref, sub)
            row = row_ref[sub]
            placed = pad_ref[member, pl.ds(SUB - row, F_ROWS), :].astype(jnp.bfloat16)
            send_ref[:, facet, slot] = placed.reshape(chans, shard, LANES)
            where_ref[(facet ^ me) * cap + slot] = VALID_BIT + row * FACET + col_ref[sub]
    for number, meta_ref in enumerate(meta_refs):
        for slot in range(cap):
            meta_ref[slot] = where_ref[number * cap + slot]


def pick_kernel(facets, cap, *refs):
    meta_in, model_ref, columns_in, rows_in, *refs = refs
    back_out, refs = refs[:facets], refs[facets:]
    meta_ref, columns_ref, rows_ref, back_ref, list_ref, sems, out_sems, *wide_refs = refs
    slots = facets * cap
    loads = start([(meta_in, meta_ref), (columns_in, columns_ref), (rows_in, rows_ref)], sems)
    loads[0].wait()
    found = 0
    for source in range(facets):
        values = [meta_ref[source * cap + slot] for slot in range(cap)]
        for slot, packed in enumerate(values):
            list_ref[found] = (packed & (VALID_BIT - 1)) * slots + source * cap + slot
            found = found + (packed >= VALID_BIT).astype(jnp.int32)
    for load in loads[1:]:
        load.wait()
    low_lanes = lax.broadcasted_iota(jnp.int32, (SUB, LANES), 1) < SUB

    def columns_of(position, wide_ref):
        entry = list_ref[position]
        where = lax.div(entry, slots)
        col = where & (FACET - 1)
        block = jnp.minimum(lax.div(col, LANES), FACET // LANES - 2)
        slab = model_ref[:, pl.ds(pl.multiple_of(block * LANES, LANES), 2 * LANES)]
        table = columns_ref[pl.ds(SPAN - col + block * LANES, 2 * LANES), :]
        wide_ref[...] = jnp.dot(
            slab, table.astype(jnp.bfloat16), preferred_element_type=jnp.float32
        )
        return lax.rem(entry, slots), lax.div(where, FACET)

    def rows_of(row, wide_ref):
        half = wide_ref[pl.ds(2 * row, 2 * SUB), :].astype(jnp.bfloat16)
        return jnp.dot(rows_ref[...], half, preferred_element_type=jnp.float32)

    def finish(image):
        turned = pltpu.roll(image[SUB:], SUB, 1)
        return (image[:SUB] + jnp.where(low_lanes, -turned, turned)).astype(jnp.bfloat16)

    def one_group(group, carry):
        places = [
            columns_of(jnp.minimum(group * PICK_GROUP + member, found - 1), wide_refs[member])
            for member in range(PICK_GROUP)
        ]
        images = [rows_of(row, wide_refs[member]) for member, (_, row) in enumerate(places)]
        images = [finish(image) for image in images]
        for (index, _), image in zip(places, images):
            back_ref[index] = image
        return carry

    lax.fori_loop(0, lax.div(found + PICK_GROUP - 1, PICK_GROUP), one_group, 0)
    fetch(
        [
            (back_ref.at[pl.ds(number * cap, cap)], back_out[number])
            for number in range(facets)
        ],
        out_sems,
    )


def add_kernel(
    facets, chans, cap, meta_in, recv_in, image_ref, meta_ref, recv_ref, sems, *canvas_refs
):
    shard = F_ROWS // chans
    facet, chan = lax.axis_index("facet"), lax.axis_index("chan")
    span = chans // PARTS
    group = span * facets * cap
    groups = [pl.ds((number ^ lax.div(chan, span)) * group, group) for number in range(PARTS)]
    loads = start(
        [(meta_in, meta_ref)] + [(recv_in.at[part], recv_ref.at[part]) for part in groups], sems
    )
    for canvas_ref in canvas_refs:
        canvas_ref[...] = jnp.zeros_like(canvas_ref)
    loads[0].wait()
    lanes = lax.broadcasted_iota(jnp.int32, (shard, LANES), 1)
    within = lanes & (SUB - 1)

    def load(packed, index):
        col = jnp.where(packed >= VALID_BIT, packed & (FACET - 1), FACET + SUB)
        shift = col & (SUB - 1)
        turned = recv_ref[index].astype(jnp.float32)
        near = jnp.where(within >= shift, turned, 0.0)
        return lax.div(col, SUB) * LANES, near, jnp.where(within >= shift, 0.0, turned)

    def one_source(source, carry):
        number = lax.div(source, facets)
        first = ((number ^ chan) * facets + ((source & (facets - 1)) ^ facet)) * cap
        place = source * cap
        packs = [meta_ref[place + slot] for slot in range(cap)]
        loaded = [load(packed, first + slot) for slot, packed in enumerate(packs)]
        for slot, (start, near, far) in enumerate(loaded):
            canvas_ref = canvas_refs[slot % CANVASES]
            place = pl.ds(pl.multiple_of(start, LANES), 2 * LANES)
            canvas_ref[:, place] += jnp.concatenate([near, far], 1)
        return carry

    sources = span * facets
    for number in range(PARTS):
        loads[1 + number].wait()
        lax.fori_loop(number * sources, (number + 1) * sources, one_source, 0, unroll=8)
    for block in range(FACET // LANES):
        first, second = [
            sum(ref[:, (2 * block + half) * LANES : (2 * block + half + 1) * LANES] for ref in canvas_refs)
            for half in range(2)
        ]
        place = slice(block * LANES, (block + 1) * LANES)
        image_ref[:, 0, place] = jnp.where(lanes < SUB, first, second)
        image_ref[:, 1, place] = pltpu.roll(jnp.where(lanes < SUB, second, first), SUB, 1)


def degrid_kernel(facets, facet_in, count_in, vis_in, coord_in, *refs):
    back_in, refs = refs[:facets], refs[facets:]
    out_ref, facet_ref, count_ref, vis_ref, coord_ref, back_ref, used_ref, sems = refs
    subs = vis_ref.shape[0]
    fetch(
        [
            (facet_in, facet_ref),
            (count_in, count_ref),
            (vis_in, vis_ref),
            (coord_in, coord_ref),
        ]
        + [(back_in[number], back_ref.at[number]) for number in range(facets)],
        sems,
    )
    me = lax.axis_index("facet")
    clear_used(used_ref, facets)
    low_lanes = lax.broadcasted_iota(jnp.int32, (SUB, LANES), 1) < SUB

    def one_group(group, carry):
        for member in range(GROUP):
            sub = group * GROUP + member
            facet, slot = next_slot(facet_ref, used_ref, sub)
            kernel_u = gaussian(coord_ref[sub, 0:1, :]).astype(jnp.bfloat16).astype(jnp.float32)
            kernel_v = gaussian(coord_ref[sub, 1:2, :]).astype(jnp.bfloat16)
            grid = back_ref[facet ^ me, slot].astype(jnp.float32)
            split = jnp.concatenate(
                [jnp.where(low_lanes, grid, 0.0), jnp.where(low_lanes, 0.0, grid)], 0
            ).astype(jnp.bfloat16)
            lines = jnp.dot(
                split,
                jnp.concatenate([kernel_v, kernel_v], 0),
                preferred_element_type=jnp.float32,
            )
            live = live_row(count_ref[sub])
            for part in range(2):
                predicted = jnp.sum(
                    lines[part * SUB : (part + 1) * SUB] * kernel_u, 0, keepdims=True
                )
                seen = vis_ref[sub, part : part + 1, :]
                out_ref[sub, part : part + 1, :] = jnp.where(live, seen - predicted, 0.0)
        return carry

    lax.fori_loop(0, subs // GROUP, one_group, 0)


def smem():
    return pl.BlockSpec(memory_space=pltpu.SMEM)


def vmem():
    return pl.BlockSpec(memory_space=pltpu.VMEM)


def hbm():
    return pl.BlockSpec(memory_space=pltpu.HBM)


def params():
    return pltpu.CompilerParams(vmem_limit_bytes=VMEM_LIMIT)


def copy_sems(count):
    return pltpu.SemaphoreType.DMA((count,))


def in_hbm(values):
    return pltpu.with_memory_space_constraint(values, pltpu.HBM)


def partner(values, axis, bit):
    return lax.ppermute(
        values, axis, [(index, index ^ bit) for index in range(lax.axis_size(axis))]
    )


def per_device(
    visibility, uv_coords, vis_count, subgrid_facet, row_offset, col_offset, model_facet
):
    facets = lax.axis_size("facet")
    chans = lax.axis_size("chan")
    subs = visibility.shape[0]
    cap = max(2, 2 * subs // facets)
    shard = F_ROWS // chans
    slots = facets * cap
    total = slots * chans
    facet_ids = subgrid_facet[:, 0]

    grid_inputs = (
        facet_ids, row_offset, col_offset, vis_count, visibility, uv_coords, forward_table()
    )
    send, *metas = pl.pallas_call(
        functools.partial(grid_kernel, facets, chans),
        out_shape=tuple(
            [jax.ShapeDtypeStruct((chans, facets, cap, shard, LANES), jnp.bfloat16)]
            + [jax.ShapeDtypeStruct((WORDS,), jnp.int32)] * facets
        ),
        in_specs=[hbm()] * 7,
        out_specs=tuple([vmem()] + [smem()] * facets),
        scratch_shapes=[
            pltpu.SMEM((subs,), jnp.int32),
            pltpu.SMEM((subs,), jnp.int32),
            pltpu.SMEM((subs,), jnp.int32),
            pltpu.SMEM((subs,), jnp.int32),
            pltpu.VMEM((subs, 2, NV), jnp.float32),
            pltpu.VMEM((subs, 2, NV), jnp.float32),
            pltpu.VMEM((LANES, LANES), jnp.bfloat16),
            pltpu.VMEM((subs, LANES, LANES), jnp.bfloat16),
            pltpu.VMEM((subs * SUB, LANES), jnp.bfloat16),
            pltpu.VMEM((GROUP, 3 * SUB, LANES), jnp.float32),
            pltpu.SMEM((facets,), jnp.int32),
            pltpu.SMEM((slots,), jnp.int32),
            copy_sems(7),
        ],
        compiler_params=params(),
        name="grid",
    )(*[in_hbm(value) for value in grid_inputs])
    metas = metas[:1] + [partner(metas[bit], "facet", bit) for bit in range(1, facets)]
    mine = jnp.concatenate([values[:cap] for values in metas])
    listed = jnp.pad(mine, (0, WORDS - slots))
    every = mine
    bit = 1
    while 2 * bit < chans:
        every = jnp.concatenate([every, partner(every, "chan", bit)])
        bit *= 2
    rest = partner(every, "chan", bit)

    send, model_facet = lax.optimization_barrier((send, model_facet))
    send = send.reshape(chans * facets, cap, shard, LANES)
    recv = lax.all_to_all(send, ("chan", "facet"), split_axis=0, concat_axis=0, tiled=True)

    columns, rows = inverse_tables()
    model = model_facet.reshape(2 * F_ROWS, FACET)
    back = pl.pallas_call(
        functools.partial(pick_kernel, facets, cap),
        out_shape=tuple([jax.ShapeDtypeStruct((cap, SUB, LANES), jnp.bfloat16)] * facets),
        in_specs=[hbm(), vmem(), hbm(), hbm()],
        out_specs=tuple([hbm()] * facets),
        scratch_shapes=[
            pltpu.SMEM((WORDS,), jnp.int32),
            pltpu.VMEM((2 * SPAN + SUB, LANES), jnp.float32),
            pltpu.VMEM((2 * SUB, 2 * SUB), jnp.bfloat16),
            pltpu.VMEM((slots, SUB, LANES), jnp.bfloat16),
            pltpu.SMEM((slots + 1,), jnp.int32),
            copy_sems(3),
            copy_sems(facets),
        ]
        + [pltpu.VMEM((2 * F_ROWS, LANES), jnp.float32)] * PICK_GROUP,
        compiler_params=params(),
        name="pick",
    )(listed, model, in_hbm(columns), in_hbm(rows))
    returned = [back[0]] + [partner(back[bit], "facet", bit) for bit in range(1, facets)]

    residual_vis = pl.pallas_call(
        functools.partial(degrid_kernel, facets),
        out_shape=jax.ShapeDtypeStruct((subs, 2, NV), jnp.float32),
        in_specs=[hbm()] * (4 + facets),
        out_specs=vmem(),
        scratch_shapes=[
            pltpu.SMEM((subs,), jnp.int32),
            pltpu.SMEM((subs,), jnp.int32),
            pltpu.VMEM((subs, 2, NV), jnp.float32),
            pltpu.VMEM((subs, 2, NV), jnp.float32),
            pltpu.VMEM((facets, cap, SUB, LANES), jnp.bfloat16),
            pltpu.SMEM((facets,), jnp.int32),
            copy_sems(4 + facets),
        ],
        compiler_params=params(),
        name="degrid",
    )(*[in_hbm(value) for value in (facet_ids, vis_count, visibility, uv_coords)], *returned)

    every, rest, residual_vis = lax.optimization_barrier((every, rest, residual_vis))
    facet_image = pl.pallas_call(
        functools.partial(add_kernel, facets, chans, cap),
        out_shape=jax.ShapeDtypeStruct((shard, 2, FACET), jnp.float32),
        in_specs=[hbm(), hbm()],
        out_specs=vmem(),
        scratch_shapes=[
            pltpu.SMEM((total,), jnp.int32),
            pltpu.VMEM((total, shard, LANES), jnp.bfloat16),
            copy_sems(1 + PARTS),
        ]
        + [pltpu.VMEM((shard, 2 * FACET + 3 * LANES), jnp.float32)] * CANVASES,
        compiler_params=params(),
        name="add",
    )(jnp.concatenate([every, rest]), recv.reshape(total, shard, LANES))
    return (facet_image[None], residual_vis)


def solution(mesh):
    in_specs = (
        P(("facet", "chan"), None, None),
        P(("facet", "chan"), None, None),
        P(("facet", "chan")),
        P(("facet", "chan"), None),
        P(("facet", "chan")),
        P(("facet", "chan")),
        P("facet", None, None, None),
    )
    out_specs = (P("facet", "chan", None, None), P(("facet", "chan"), None, None))
    return jax.shard_map(
        per_device, mesh=mesh, in_specs=in_specs, out_specs=out_specs, check_vma=False
    )
```

```python
import functools
import math

import jax
import jax.numpy as jnp
import numpy as np
from jax import lax
from jax.experimental import pallas as pl
from jax.experimental.pallas import tpu as pltpu
from jax.sharding import PartitionSpec as P

SUB = 64
FACET = 4096
F_ROWS = 128
NV = 512
LANES = 128
VALID_BIT = 1 << 20
GROUP = 4
WORDS = 128

SPAN = 3 * SUB
PICK_GROUP = 16
CANVASES = 2
PARTS = 4

VMEM_LIMIT = 48 * 1024 * 1024


def dft_arrays():
    index_line = np.arange(SUB)
    phase = (index_line[:, None] * index_line[None, :]) % SUB
    angle = (2.0 * math.pi * phase / SUB).astype(np.float32)
    cos_table = np.cos(angle) / np.float32(math.sqrt(SUB))
    sin_table = -np.sin(angle) / np.float32(math.sqrt(SUB))
    return cos_table.astype(np.float32), sin_table.astype(np.float32)


def forward_table():
    cos_table, sin_table = dft_arrays()
    right = np.concatenate(
        [np.concatenate([cos_table, sin_table], 1), np.concatenate([-sin_table, cos_table], 1)], 0
    )
    return jnp.asarray(right, jnp.bfloat16)


def inverse_tables():
    cos_table, sin_table = dft_arrays()
    sin_table = -sin_table
    columns = np.zeros((2 * SPAN + SUB, LANES), np.float32)
    columns[SPAN : SPAN + SUB] = np.concatenate([cos_table, sin_table], 1)
    rows = np.zeros((2 * SUB, 2 * SUB), np.float32)
    rows[:SUB, 0::2] = cos_table
    rows[:SUB, 1::2] = -sin_table
    rows[SUB:, 0::2] = sin_table
    rows[SUB:, 1::2] = cos_table
    columns = columns.astype(jnp.bfloat16).astype(np.float32)
    return jnp.asarray(columns), jnp.asarray(rows, jnp.bfloat16)


def gaussian(coord_row):
    pixel = lax.broadcasted_iota(jnp.int32, (SUB, NV), 0).astype(jnp.float32)
    delta = pixel - coord_row
    return jnp.exp(-(delta * delta))


def live_row(count):
    return lax.broadcasted_iota(jnp.int32, (1, NV), 1) < count


def start(copies, sems):
    started = [
        pltpu.make_async_copy(source, target, sems.at[number])
        for number, (source, target) in enumerate(copies)
    ]
    for copy in started:
        copy.start()
    return started


def fetch(copies, sems):
    for copy in start(copies, sems):
        copy.wait()


def next_slot(facet_ref, used_ref, sub):
    facet = facet_ref[sub]
    slot = used_ref[facet]
    used_ref[facet] = slot + 1
    return facet, slot


def clear_used(used_ref, facets):
    for facet in range(facets):
        used_ref[facet] = 0


def grid_kernel(
    facets, chans, facet_in, row_in, col_in, count_in, vis_in, coord_in, right_in, send_ref, *refs
):
    meta_refs, refs = refs[:facets], refs[facets:]
    facet_ref, row_ref, col_ref, count_ref, vis_ref, coord_ref, right_ref, *refs = refs
    stack_ref, half_ref, pad_ref, used_ref, where_ref, sems = refs
    me = lax.axis_index("facet")
    cap = send_ref.shape[2]
    subs = vis_ref.shape[0]
    shard = F_ROWS // chans
    fetch(
        [
            (facet_in, facet_ref),
            (row_in, row_ref),
            (col_in, col_ref),
            (count_in, count_ref),
            (vis_in, vis_ref),
            (coord_in, coord_ref),
            (right_in, right_ref),
        ],
        sems,
    )
    clear_used(used_ref, facets)
    for index in range(facets * cap):
        where_ref[index] = 0
    for member in range(GROUP):
        pad_ref[member, :SUB, :] = jnp.zeros((SUB, LANES), jnp.float32)
        pad_ref[member, 2 * SUB :, :] = jnp.zeros((SUB, LANES), jnp.float32)
    low_lanes = lax.broadcasted_iota(jnp.int32, (SUB, LANES), 1) < SUB

    def grid_one(sub):
        kernel_u = gaussian(coord_ref[sub, 0:1, :]).astype(jnp.bfloat16)
        kernel_v = gaussian(coord_ref[sub, 1:2, :])
        live = live_row(count_ref[sub])
        spread = jnp.concatenate(
            [
                (jnp.where(live, vis_ref[sub, part : part + 1, :], 0.0) * kernel_v).astype(
                    jnp.bfloat16
                )
                for part in range(2)
            ],
            0,
        )
        gridded = lax.dot_general(
            kernel_u, spread, (((1,), (1,)), ((), ())), preferred_element_type=jnp.float32
        )
        swapped = pltpu.roll(gridded, SUB, 1)
        swapped = jnp.where(low_lanes, -swapped, swapped)
        stack_ref[sub] = jnp.concatenate([gridded, swapped], 0).astype(jnp.bfloat16)

    def grid_group(group, carry):
        for member in range(GROUP):
            grid_one(group * GROUP + member)
        return carry

    lax.fori_loop(0, subs // GROUP, grid_group, 0, unroll=True)
    for sub in range(subs):
        half_ref[sub * SUB : (sub + 1) * SUB, :] = jnp.dot(
            right_ref[:SUB, :], stack_ref[sub], preferred_element_type=jnp.float32
        ).astype(jnp.bfloat16)

    for group in range(subs // GROUP):
        base = group * GROUP
        patches = jnp.dot(
            half_ref[base * SUB : (base + GROUP) * SUB, :],
            right_ref[...],
            preferred_element_type=jnp.float32,
        )
        for member in range(GROUP):
            patch = patches[member * SUB : (member + 1) * SUB]
            turned = pltpu.roll(patch, col_ref[base + member] & (LANES - 1), 1)
            pad_ref[member, SUB : 2 * SUB, :] = turned
        for member in range(GROUP):
            sub = base + member
            facet, slot = next_slot(facet_ref, used_ref, sub)
            row = row_ref[sub]
            placed = pad_ref[member, pl.ds(SUB - row, F_ROWS), :].astype(jnp.bfloat16)
            send_ref[:, facet, slot] = placed.reshape(chans, shard, LANES)
            where_ref[(facet ^ me) * cap + slot] = VALID_BIT + row * FACET + col_ref[sub]
    for number, meta_ref in enumerate(meta_refs):
        for slot in range(cap):
            meta_ref[slot] = where_ref[number * cap + slot]


def pick_kernel(facets, cap, *refs):
    meta_in, model_ref, columns_in, rows_in, *refs = refs
    back_refs, refs = refs[:facets], refs[facets:]
    meta_ref, columns_ref, rows_ref, back_ref, list_ref, sems, *wide_refs = refs
    slots = facets * cap
    loads = start([(meta_in, meta_ref), (columns_in, columns_ref), (rows_in, rows_ref)], sems)
    loads[0].wait()
    found = 0
    for source in range(facets):
        values = [meta_ref[source * cap + slot] for slot in range(cap)]
        for slot, packed in enumerate(values):
            list_ref[found] = (packed & (VALID_BIT - 1)) * slots + source * cap + slot
            found = found + (packed >= VALID_BIT).astype(jnp.int32)
    for load in loads[1:]:
        load.wait()
    low_lanes = lax.broadcasted_iota(jnp.int32, (SUB, LANES), 1) < SUB

    def columns_of(position, wide_ref):
        entry = list_ref[position]
        where = lax.div(entry, slots)
        col = where & (FACET - 1)
        block = jnp.minimum(lax.div(col, LANES), FACET // LANES - 2)
        slab = model_ref[:, pl.ds(pl.multiple_of(block * LANES, LANES), 2 * LANES)]
        table = columns_ref[pl.ds(SPAN - col + block * LANES, 2 * LANES), :]
        wide_ref[...] = jnp.dot(
            slab, table.astype(jnp.bfloat16), preferred_element_type=jnp.float32
        )
        return lax.rem(entry, slots), lax.div(where, FACET)

    def rows_of(row, wide_ref):
        half = wide_ref[pl.ds(2 * row, 2 * SUB), :].astype(jnp.bfloat16)
        return jnp.dot(rows_ref[...], half, preferred_element_type=jnp.float32)

    def finish(image):
        turned = pltpu.roll(image[SUB:], SUB, 1)
        return (image[:SUB] + jnp.where(low_lanes, -turned, turned)).astype(jnp.bfloat16)

    def windows(first, count):
        places = [
            columns_of(jnp.minimum(first + member, found - 1), wide_refs[member])
            for member in range(count)
        ]
        images = [rows_of(row, wide_refs[member]) for member, (_, row) in enumerate(places)]
        images = [finish(image) for image in images]
        for (index, _), image in zip(places, images):
            back_ref[index] = image

    def one_group(group, carry):
        windows(group * PICK_GROUP, PICK_GROUP)
        return carry

    half = PICK_GROUP // 2
    whole = lax.div(found, PICK_GROUP)
    rest = found - whole * PICK_GROUP
    lax.fori_loop(0, whole, one_group, 0)
    pl.when(rest > half)(lambda: windows(whole * PICK_GROUP, PICK_GROUP))
    pl.when((rest > 0) & (rest <= half))(lambda: windows(whole * PICK_GROUP, half))
    for number in range(facets):
        back_refs[number][...] = back_ref[number * cap : (number + 1) * cap]


def add_kernel(
    facets, chans, cap, meta_in, recv_in, image_ref, meta_ref, recv_ref, sems, *canvas_refs
):
    shard = F_ROWS // chans
    facet, chan = lax.axis_index("facet"), lax.axis_index("chan")
    span = chans // PARTS
    group = span * facets * cap
    groups = [pl.ds((number ^ lax.div(chan, span)) * group, group) for number in range(PARTS)]
    loads = start(
        [(meta_in, meta_ref)] + [(recv_in.at[part], recv_ref.at[part]) for part in groups], sems
    )
    for canvas_ref in canvas_refs:
        canvas_ref[...] = jnp.zeros_like(canvas_ref)
    loads[0].wait()
    lanes = lax.broadcasted_iota(jnp.int32, (shard, LANES), 1)
    within = lanes & (SUB - 1)

    def load(packed, index):
        col = jnp.where(packed >= VALID_BIT, packed & (FACET - 1), FACET + SUB)
        shift = col & (SUB - 1)
        turned = recv_ref[index].astype(jnp.float32)
        near = jnp.where(within >= shift, turned, 0.0)
        return lax.div(col, SUB) * LANES, near, jnp.where(within >= shift, 0.0, turned)

    def one_source(source, carry):
        number = lax.div(source, facets)
        first = ((number ^ chan) * facets + ((source & (facets - 1)) ^ facet)) * cap
        place = source * cap
        packs = [meta_ref[place + slot] for slot in range(cap)]
        loaded = [load(packed, first + slot) for slot, packed in enumerate(packs)]
        for slot, (start, near, far) in enumerate(loaded):
            canvas_ref = canvas_refs[slot % CANVASES]
            place = pl.ds(pl.multiple_of(start, LANES), 2 * LANES)
            canvas_ref[:, place] += jnp.concatenate([near, far], 1)
        return carry

    sources = span * facets
    for number in range(PARTS):
        loads[1 + number].wait()
        lax.fori_loop(number * sources, (number + 1) * sources, one_source, 0, unroll=8)
    for block in range(FACET // LANES):
        first, second = [
            sum(ref[:, (2 * block + half) * LANES : (2 * block + half + 1) * LANES] for ref in canvas_refs)
            for half in range(2)
        ]
        place = slice(block * LANES, (block + 1) * LANES)
        image_ref[:, 0, place] = jnp.where(lanes < SUB, first, second)
        image_ref[:, 1, place] = pltpu.roll(jnp.where(lanes < SUB, second, first), SUB, 1)


def degrid_kernel(facets, facet_in, count_in, vis_in, coord_in, *refs):
    back_in, refs = refs[:facets], refs[facets:]
    out_ref, facet_ref, count_ref, vis_ref, coord_ref, back_ref, used_ref, sems = refs
    subs = vis_ref.shape[0]
    loads = start(
        [
            (facet_in, facet_ref),
            (count_in, count_ref),
            (vis_in, vis_ref),
            (coord_in, coord_ref),
        ],
        sems,
    )
    for number in range(facets):
        back_ref[number] = back_in[number][...]
    for load in loads:
        load.wait()
    me = lax.axis_index("facet")
    clear_used(used_ref, facets)
    low_lanes = lax.broadcasted_iota(jnp.int32, (SUB, LANES), 1) < SUB

    def one_group(group, carry):
        for member in range(GROUP):
            sub = group * GROUP + member
            facet, slot = next_slot(facet_ref, used_ref, sub)
            kernel_u = gaussian(coord_ref[sub, 0:1, :]).astype(jnp.bfloat16).astype(jnp.float32)
            kernel_v = gaussian(coord_ref[sub, 1:2, :]).astype(jnp.bfloat16)
            grid = back_ref[facet ^ me, slot].astype(jnp.float32)
            split = jnp.concatenate(
                [jnp.where(low_lanes, grid, 0.0), jnp.where(low_lanes, 0.0, grid)], 0
            ).astype(jnp.bfloat16)
            lines = jnp.dot(
                split,
                jnp.concatenate([kernel_v, kernel_v], 0),
                preferred_element_type=jnp.float32,
            )
            live = live_row(count_ref[sub])
            for part in range(2):
                predicted = jnp.sum(
                    lines[part * SUB : (part + 1) * SUB] * kernel_u, 0, keepdims=True
                )
                seen = vis_ref[sub, part : part + 1, :]
                out_ref[sub, part : part + 1, :] = jnp.where(live, seen - predicted, 0.0)
        return carry

    lax.fori_loop(0, subs // GROUP, one_group, 0, unroll=2)


def smem():
    return pl.BlockSpec(memory_space=pltpu.SMEM)


def vmem():
    return pl.BlockSpec(memory_space=pltpu.VMEM)


def hbm():
    return pl.BlockSpec(memory_space=pltpu.HBM)


def params():
    return pltpu.CompilerParams(vmem_limit_bytes=VMEM_LIMIT)


def copy_sems(count):
    return pltpu.SemaphoreType.DMA((count,))


def in_hbm(values):
    return pltpu.with_memory_space_constraint(values, pltpu.HBM)


def partner(values, axis, bit):
    return lax.ppermute(
        values, axis, [(index, index ^ bit) for index in range(lax.axis_size(axis))]
    )


def per_device(
    visibility, uv_coords, vis_count, subgrid_facet, row_offset, col_offset, model_facet
):
    facets = lax.axis_size("facet")
    chans = lax.axis_size("chan")
    subs = visibility.shape[0]
    cap = max(2, 2 * subs // facets)
    shard = F_ROWS // chans
    slots = facets * cap
    total = slots * chans
    facet_ids = subgrid_facet[:, 0]

    grid_inputs = (
        facet_ids, row_offset, col_offset, vis_count, visibility, uv_coords, forward_table()
    )
    send, *metas = pl.pallas_call(
        functools.partial(grid_kernel, facets, chans),
        out_shape=tuple(
            [jax.ShapeDtypeStruct((chans, facets, cap, shard, LANES), jnp.bfloat16)]
            + [jax.ShapeDtypeStruct((WORDS,), jnp.int32)] * facets
        ),
        in_specs=[hbm()] * 7,
        out_specs=tuple([vmem()] + [smem()] * facets),
        scratch_shapes=[
            pltpu.SMEM((subs,), jnp.int32),
            pltpu.SMEM((subs,), jnp.int32),
            pltpu.SMEM((subs,), jnp.int32),
            pltpu.SMEM((subs,), jnp.int32),
            pltpu.VMEM((subs, 2, NV), jnp.float32),
            pltpu.VMEM((subs, 2, NV), jnp.float32),
            pltpu.VMEM((LANES, LANES), jnp.bfloat16),
            pltpu.VMEM((subs, LANES, LANES), jnp.bfloat16),
            pltpu.VMEM((subs * SUB, LANES), jnp.bfloat16),
            pltpu.VMEM((GROUP, 3 * SUB, LANES), jnp.float32),
            pltpu.SMEM((facets,), jnp.int32),
            pltpu.SMEM((slots,), jnp.int32),
            copy_sems(7),
        ],
        compiler_params=params(),
        name="grid",
    )(*[in_hbm(value) for value in grid_inputs])
    metas = metas[:1] + [partner(metas[bit], "facet", bit) for bit in range(1, facets)]
    mine = jnp.concatenate([values[:cap] for values in metas])
    listed = jnp.pad(mine, (0, WORDS - slots))
    every = mine
    bit = 1
    while 2 * bit < chans:
        every = jnp.concatenate([every, partner(every, "chan", bit)])
        bit *= 2
    rest = partner(every, "chan", bit)

    send, model_facet = lax.optimization_barrier((send, model_facet))
    send = send.reshape(chans * facets, cap, shard, LANES)
    recv = lax.all_to_all(send, ("chan", "facet"), split_axis=0, concat_axis=0, tiled=True)

    columns, rows = inverse_tables()
    model = model_facet.reshape(2 * F_ROWS, FACET)
    back = pl.pallas_call(
        functools.partial(pick_kernel, facets, cap),
        out_shape=tuple([jax.ShapeDtypeStruct((cap, SUB, LANES), jnp.bfloat16)] * facets),
        in_specs=[hbm(), vmem(), hbm(), hbm()],
        out_specs=tuple([vmem()] * facets),
        scratch_shapes=[
            pltpu.SMEM((WORDS,), jnp.int32),
            pltpu.VMEM((2 * SPAN + SUB, LANES), jnp.float32),
            pltpu.VMEM((2 * SUB, 2 * SUB), jnp.bfloat16),
            pltpu.VMEM((slots, SUB, LANES), jnp.bfloat16),
            pltpu.SMEM((slots + 1,), jnp.int32),
            copy_sems(3),
        ]
        + [pltpu.VMEM((2 * F_ROWS, LANES), jnp.float32)] * PICK_GROUP,
        compiler_params=params(),
        name="pick",
    )(listed, model, in_hbm(columns), in_hbm(rows))
    returned = [back[0]] + [partner(back[bit], "facet", bit) for bit in range(1, facets)]

    residual_vis = pl.pallas_call(
        functools.partial(degrid_kernel, facets),
        out_shape=jax.ShapeDtypeStruct((subs, 2, NV), jnp.float32),
        in_specs=[hbm()] * 4 + [vmem()] * facets,
        out_specs=vmem(),
        scratch_shapes=[
            pltpu.SMEM((subs,), jnp.int32),
            pltpu.SMEM((subs,), jnp.int32),
            pltpu.VMEM((subs, 2, NV), jnp.float32),
            pltpu.VMEM((subs, 2, NV), jnp.float32),
            pltpu.VMEM((facets, cap, SUB, LANES), jnp.bfloat16),
            pltpu.SMEM((facets,), jnp.int32),
            copy_sems(4),
        ],
        compiler_params=params(),
        name="degrid",
    )(*[in_hbm(value) for value in (facet_ids, vis_count, visibility, uv_coords)], *returned)

    every, rest, residual_vis = lax.optimization_barrier((every, rest, residual_vis))
    facet_image = pl.pallas_call(
        functools.partial(add_kernel, facets, chans, cap),
        out_shape=jax.ShapeDtypeStruct((shard, 2, FACET), jnp.float32),
        in_specs=[hbm(), hbm()],
        out_specs=vmem(),
        scratch_shapes=[
            pltpu.SMEM((total,), jnp.int32),
            pltpu.VMEM((total, shard, LANES), jnp.bfloat16),
            copy_sems(1 + PARTS),
        ]
        + [pltpu.VMEM((shard, 2 * FACET + 3 * LANES), jnp.float32)] * CANVASES,
        compiler_params=params(),
        name="add",
    )(jnp.concatenate([every, rest]), recv.reshape(total, shard, LANES))
    return (facet_image[None], residual_vis)


def solution(mesh):
    in_specs = (
        P(("facet", "chan"), None, None),
        P(("facet", "chan"), None, None),
        P(("facet", "chan")),
        P(("facet", "chan"), None),
        P(("facet", "chan")),
        P(("facet", "chan")),
        P("facet", None, None, None),
    )
    out_specs = (P("facet", "chan", None, None), P(("facet", "chan"), None, None))
    return jax.shard_map(
        per_device, mesh=mesh, in_specs=in_specs, out_specs=out_specs, check_vma=False
    )
```

```python
import functools
import math

import jax
import jax.numpy as jnp
import numpy as np
from jax import lax
from jax.experimental import pallas as pl
from jax.experimental.pallas import tpu as pltpu
from jax.sharding import PartitionSpec as P

SUB = 64
FACET = 4096
F_ROWS = 128
NV = 512
LANES = 128
VALID_BIT = 1 << 20
GROUP = 4
WORDS = 128

SPAN = 3 * SUB
PICK_GROUP = 16
CANVASES = 2
PARTS = 4
IMAGE_PARTS = 2

VMEM_LIMIT = 48 * 1024 * 1024


def dft_arrays():
    index_line = np.arange(SUB)
    phase = (index_line[:, None] * index_line[None, :]) % SUB
    angle = (2.0 * math.pi * phase / SUB).astype(np.float32)
    cos_table = np.cos(angle) / np.float32(math.sqrt(SUB))
    sin_table = -np.sin(angle) / np.float32(math.sqrt(SUB))
    return cos_table.astype(np.float32), sin_table.astype(np.float32)


def forward_table():
    cos_table, sin_table = dft_arrays()
    right = np.concatenate(
        [np.concatenate([cos_table, sin_table], 1), np.concatenate([-sin_table, cos_table], 1)], 0
    )
    return jnp.asarray(right, jnp.bfloat16)


def inverse_tables():
    cos_table, sin_table = dft_arrays()
    sin_table = -sin_table
    columns = np.zeros((2 * SPAN + SUB, LANES), np.float32)
    columns[SPAN : SPAN + SUB] = np.concatenate([cos_table, sin_table], 1)
    rows = np.zeros((2 * SUB, 2 * SUB), np.float32)
    rows[:SUB, 0::2] = cos_table
    rows[:SUB, 1::2] = -sin_table
    rows[SUB:, 0::2] = sin_table
    rows[SUB:, 1::2] = cos_table
    columns = columns.astype(jnp.bfloat16).astype(np.float32)
    return jnp.asarray(columns), jnp.asarray(rows, jnp.bfloat16)


def gaussian(coord_row):
    pixel = lax.broadcasted_iota(jnp.int32, (SUB, NV), 0).astype(jnp.float32)
    delta = pixel - coord_row
    return jnp.exp(-(delta * delta))


def live_row(count):
    return lax.broadcasted_iota(jnp.int32, (1, NV), 1) < count


def start(copies, sems):
    started = [
        pltpu.make_async_copy(source, target, sems.at[number])
        for number, (source, target) in enumerate(copies)
    ]
    for copy in started:
        copy.start()
    return started


def fetch(copies, sems):
    for copy in start(copies, sems):
        copy.wait()


def next_slot(facet_ref, used_ref, sub):
    facet = facet_ref[sub]
    slot = used_ref[facet]
    used_ref[facet] = slot + 1
    return facet, slot


def clear_used(used_ref, facets):
    for facet in range(facets):
        used_ref[facet] = 0


def grid_kernel(
    facets, chans, facet_in, row_in, col_in, count_in, vis_in, coord_in, right_in, send_ref, *refs
):
    meta_refs, refs = refs[:facets], refs[facets:]
    facet_ref, row_ref, col_ref, count_ref, vis_ref, coord_ref, right_ref, *refs = refs
    stack_ref, half_ref, pad_ref, used_ref, where_ref, sems = refs
    me = lax.axis_index("facet")
    cap = send_ref.shape[2]
    subs = vis_ref.shape[0]
    shard = F_ROWS // chans
    loads = start(
        [
            (facet_in, facet_ref),
            (row_in, row_ref),
            (col_in, col_ref),
            (count_in, count_ref),
            (vis_in, vis_ref),
            (coord_in, coord_ref),
            (right_in, right_ref),
        ],
        sems,
    )
    clear_used(used_ref, facets)
    for index in range(facets * cap):
        where_ref[index] = 0
    for member in range(GROUP):
        pad_ref[member, :SUB, :] = jnp.zeros((SUB, LANES), jnp.float32)
        pad_ref[member, 2 * SUB :, :] = jnp.zeros((SUB, LANES), jnp.float32)
    for load in loads:
        load.wait()
    low_lanes = lax.broadcasted_iota(jnp.int32, (SUB, LANES), 1) < SUB

    def grid_one(sub):
        kernel_u = gaussian(coord_ref[sub, 0:1, :]).astype(jnp.bfloat16)
        kernel_v = gaussian(coord_ref[sub, 1:2, :])
        live = live_row(count_ref[sub])
        spread = jnp.concatenate(
            [
                (jnp.where(live, vis_ref[sub, part : part + 1, :], 0.0) * kernel_v).astype(
                    jnp.bfloat16
                )
                for part in range(2)
            ],
            0,
        )
        gridded = lax.dot_general(
            kernel_u, spread, (((1,), (1,)), ((), ())), preferred_element_type=jnp.float32
        )
        swapped = pltpu.roll(gridded, SUB, 1)
        swapped = jnp.where(low_lanes, -swapped, swapped)
        stack_ref[sub] = jnp.concatenate([gridded, swapped], 0).astype(jnp.bfloat16)

    def grid_group(group, carry):
        for member in range(GROUP):
            grid_one(group * GROUP + member)
        return carry

    lax.fori_loop(0, subs // GROUP, grid_group, 0, unroll=True)
    for sub in range(subs):
        half_ref[sub * SUB : (sub + 1) * SUB, :] = jnp.dot(
            right_ref[:SUB, :], stack_ref[sub], preferred_element_type=jnp.float32
        ).astype(jnp.bfloat16)

    for group in range(subs // GROUP):
        base = group * GROUP
        patches = jnp.dot(
            half_ref[base * SUB : (base + GROUP) * SUB, :],
            right_ref[...],
            preferred_element_type=jnp.float32,
        )
        for member in range(GROUP):
            patch = patches[member * SUB : (member + 1) * SUB]
            turned = pltpu.roll(patch, col_ref[base + member] & (LANES - 1), 1)
            pad_ref[member, SUB : 2 * SUB, :] = turned
        for member in range(GROUP):
            sub = base + member
            facet, slot = next_slot(facet_ref, used_ref, sub)
            row = row_ref[sub]
            placed = pad_ref[member, pl.ds(SUB - row, F_ROWS), :].astype(jnp.bfloat16)
            send_ref[:, facet, slot] = placed.reshape(chans, shard, LANES)
            where_ref[(facet ^ me) * cap + slot] = VALID_BIT + row * FACET + col_ref[sub]
    for number, meta_ref in enumerate(meta_refs):
        for slot in range(cap):
            meta_ref[slot] = where_ref[number * cap + slot]


def pick_kernel(facets, cap, *refs):
    meta_in, model_ref, columns_in, rows_in, *refs = refs
    back_refs, refs = refs[:facets], refs[facets:]
    meta_ref, columns_ref, rows_ref, back_ref, list_ref, sems, *wide_refs = refs
    slots = facets * cap
    loads = start([(meta_in, meta_ref), (columns_in, columns_ref), (rows_in, rows_ref)], sems)
    loads[0].wait()
    found = 0
    for source in range(facets):
        values = [meta_ref[source * cap + slot] for slot in range(cap)]
        for slot, packed in enumerate(values):
            list_ref[found] = (packed & (VALID_BIT - 1)) * slots + source * cap + slot
            found = found + (packed >= VALID_BIT).astype(jnp.int32)
    for load in loads[1:]:
        load.wait()
    low_lanes = lax.broadcasted_iota(jnp.int32, (SUB, LANES), 1) < SUB

    def columns_of(position, wide_ref):
        entry = list_ref[position]
        where = lax.div(entry, slots)
        col = where & (FACET - 1)
        block = jnp.minimum(lax.div(col, LANES), FACET // LANES - 2)
        slab = model_ref[:, pl.ds(pl.multiple_of(block * LANES, LANES), 2 * LANES)]
        table = columns_ref[pl.ds(SPAN - col + block * LANES, 2 * LANES), :]
        wide_ref[...] = jnp.dot(
            slab, table.astype(jnp.bfloat16), preferred_element_type=jnp.float32
        )
        return lax.rem(entry, slots), lax.div(where, FACET)

    def rows_of(row, wide_ref):
        half = wide_ref[pl.ds(2 * row, 2 * SUB), :].astype(jnp.bfloat16)
        return jnp.dot(rows_ref[...], half, preferred_element_type=jnp.float32)

    def finish(image):
        turned = pltpu.roll(image[SUB:], SUB, 1)
        return (image[:SUB] + jnp.where(low_lanes, -turned, turned)).astype(jnp.bfloat16)

    def windows(first, count):
        places = [
            columns_of(jnp.minimum(first + member, found - 1), wide_refs[member])
            for member in range(count)
        ]
        images = [rows_of(row, wide_refs[member]) for member, (_, row) in enumerate(places)]
        images = [finish(image) for image in images]
        for (index, _), image in zip(places, images):
            back_ref[index] = image

    def one_group(group, carry):
        windows(group * PICK_GROUP, PICK_GROUP)
        return carry

    half = PICK_GROUP // 2
    whole = lax.div(found, PICK_GROUP)
    rest = found - whole * PICK_GROUP
    lax.fori_loop(0, whole, one_group, 0)
    pl.when(rest > half)(lambda: windows(whole * PICK_GROUP, PICK_GROUP))
    pl.when((rest > 0) & (rest <= half))(lambda: windows(whole * PICK_GROUP, half))
    for number in range(facets):
        back_refs[number][...] = back_ref[number * cap : (number + 1) * cap]


def add_kernel(
    facets, chans, cap, meta_in, recv_in, image_out, meta_ref, recv_ref, image_ref, sems, out_sems,
    *canvas_refs,
):
    shard = F_ROWS // chans
    facet, chan = lax.axis_index("facet"), lax.axis_index("chan")
    span = chans // PARTS
    group = span * facets * cap
    groups = [pl.ds((number ^ lax.div(chan, span)) * group, group) for number in range(PARTS)]
    loads = start(
        [(meta_in, meta_ref)] + [(recv_in.at[part], recv_ref.at[part]) for part in groups], sems
    )
    for canvas_ref in canvas_refs:
        canvas_ref[...] = jnp.zeros_like(canvas_ref)
    loads[0].wait()
    lanes = lax.broadcasted_iota(jnp.int32, (shard, LANES), 1)
    within = lanes & (SUB - 1)

    def load(packed, index):
        col = jnp.where(packed >= VALID_BIT, packed & (FACET - 1), FACET + SUB)
        shift = col & (SUB - 1)
        turned = recv_ref[index].astype(jnp.float32)
        near = jnp.where(within >= shift, turned, 0.0)
        return lax.div(col, SUB) * LANES, near, jnp.where(within >= shift, 0.0, turned)

    def one_source(source, carry):
        number = lax.div(source, facets)
        first = ((number ^ chan) * facets + ((source & (facets - 1)) ^ facet)) * cap
        place = source * cap
        packs = [meta_ref[place + slot] for slot in range(cap)]
        loaded = [load(packed, first + slot) for slot, packed in enumerate(packs)]
        for slot, (start, near, far) in enumerate(loaded):
            canvas_ref = canvas_refs[slot % CANVASES]
            place = pl.ds(pl.multiple_of(start, LANES), 2 * LANES)
            canvas_ref[:, place] += jnp.concatenate([near, far], 1)
        return carry

    sources = span * facets
    for number in range(PARTS):
        loads[1 + number].wait()
        lax.fori_loop(number * sources, (number + 1) * sources, one_source, 0, unroll=8)
    blocks = FACET // LANES
    stores = []
    for block in range(blocks):
        first, second = [
            sum(ref[:, (2 * block + half) * LANES : (2 * block + half + 1) * LANES] for ref in canvas_refs)
            for half in range(2)
        ]
        place = slice(block * LANES, (block + 1) * LANES)
        image_ref[:, 0, place] = jnp.where(lanes < SUB, first, second)
        image_ref[:, 1, place] = pltpu.roll(jnp.where(lanes < SUB, second, first), SUB, 1)
        if (block + 1) % (blocks // IMAGE_PARTS) == 0:
            number = len(stores)
            width = FACET // IMAGE_PARTS
            part = pl.ds(number * width, width)
            stores.append(
                pltpu.make_async_copy(
                    image_ref.at[:, :, part], image_out.at[:, :, part], out_sems.at[number]
                )
            )
            stores[-1].start()
    for store in stores:
        store.wait()


def degrid_kernel(facets, facet_in, count_in, vis_in, coord_in, *refs):
    back_in, refs = refs[:facets], refs[facets:]
    out_ref, facet_ref, count_ref, vis_ref, coord_ref, back_ref, used_ref, sems = refs
    subs = vis_ref.shape[0]
    loads = start(
        [
            (facet_in, facet_ref),
            (count_in, count_ref),
            (vis_in, vis_ref),
            (coord_in, coord_ref),
        ],
        sems,
    )
    for number in range(facets):
        back_ref[number] = back_in[number][...]
    for load in loads:
        load.wait()
    me = lax.axis_index("facet")
    clear_used(used_ref, facets)
    low_lanes = lax.broadcasted_iota(jnp.int32, (SUB, LANES), 1) < SUB

    def one_group(group, carry):
        for member in range(GROUP):
            sub = group * GROUP + member
            facet, slot = next_slot(facet_ref, used_ref, sub)
            kernel_u = gaussian(coord_ref[sub, 0:1, :]).astype(jnp.bfloat16).astype(jnp.float32)
            kernel_v = gaussian(coord_ref[sub, 1:2, :]).astype(jnp.bfloat16)
            grid = back_ref[facet ^ me, slot].astype(jnp.float32)
            split = jnp.concatenate(
                [jnp.where(low_lanes, grid, 0.0), jnp.where(low_lanes, 0.0, grid)], 0
            ).astype(jnp.bfloat16)
            lines = jnp.dot(
                split,
                jnp.concatenate([kernel_v, kernel_v], 0),
                preferred_element_type=jnp.float32,
            )
            live = live_row(count_ref[sub])
            for part in range(2):
                predicted = jnp.sum(
                    lines[part * SUB : (part + 1) * SUB] * kernel_u, 0, keepdims=True
                )
                seen = vis_ref[sub, part : part + 1, :]
                out_ref[sub, part : part + 1, :] = jnp.where(live, seen - predicted, 0.0)
        return carry

    lax.fori_loop(0, subs // GROUP, one_group, 0, unroll=2)


def smem():
    return pl.BlockSpec(memory_space=pltpu.SMEM)


def vmem():
    return pl.BlockSpec(memory_space=pltpu.VMEM)


def hbm():
    return pl.BlockSpec(memory_space=pltpu.HBM)


def params():
    return pltpu.CompilerParams(vmem_limit_bytes=VMEM_LIMIT)


def copy_sems(count):
    return pltpu.SemaphoreType.DMA((count,))


def in_hbm(values):
    return pltpu.with_memory_space_constraint(values, pltpu.HBM)


def partner(values, axis, bit):
    return lax.ppermute(
        values, axis, [(index, index ^ bit) for index in range(lax.axis_size(axis))]
    )


def per_device(
    visibility, uv_coords, vis_count, subgrid_facet, row_offset, col_offset, model_facet
):
    facets = lax.axis_size("facet")
    chans = lax.axis_size("chan")
    subs = visibility.shape[0]
    cap = max(2, 2 * subs // facets)
    shard = F_ROWS // chans
    slots = facets * cap
    total = slots * chans
    facet_ids = subgrid_facet[:, 0]

    grid_inputs = (
        facet_ids, row_offset, col_offset, vis_count, visibility, uv_coords, forward_table()
    )
    send, *metas = pl.pallas_call(
        functools.partial(grid_kernel, facets, chans),
        out_shape=tuple(
            [jax.ShapeDtypeStruct((chans, facets, cap, shard, LANES), jnp.bfloat16)]
            + [jax.ShapeDtypeStruct((WORDS,), jnp.int32)] * facets
        ),
        in_specs=[hbm()] * 7,
        out_specs=tuple([vmem()] + [smem()] * facets),
        scratch_shapes=[
            pltpu.SMEM((subs,), jnp.int32),
            pltpu.SMEM((subs,), jnp.int32),
            pltpu.SMEM((subs,), jnp.int32),
            pltpu.SMEM((subs,), jnp.int32),
            pltpu.VMEM((subs, 2, NV), jnp.float32),
            pltpu.VMEM((subs, 2, NV), jnp.float32),
            pltpu.VMEM((LANES, LANES), jnp.bfloat16),
            pltpu.VMEM((subs, LANES, LANES), jnp.bfloat16),
            pltpu.VMEM((subs * SUB, LANES), jnp.bfloat16),
            pltpu.VMEM((GROUP, 3 * SUB, LANES), jnp.float32),
            pltpu.SMEM((facets,), jnp.int32),
            pltpu.SMEM((slots,), jnp.int32),
            copy_sems(7),
        ],
        compiler_params=params(),
        name="grid",
    )(*[in_hbm(value) for value in grid_inputs])
    metas = metas[:1] + [partner(metas[bit], "facet", bit) for bit in range(1, facets)]
    mine = jnp.concatenate([values[:cap] for values in metas])
    listed = jnp.pad(mine, (0, WORDS - slots))
    every = mine
    bit = 1
    while 2 * bit < chans:
        every = jnp.concatenate([every, partner(every, "chan", bit)])
        bit *= 2
    rest = partner(every, "chan", bit)

    send, model_facet = lax.optimization_barrier((send, model_facet))
    send = send.reshape(chans * facets, cap, shard, LANES)
    recv = lax.all_to_all(send, ("chan", "facet"), split_axis=0, concat_axis=0, tiled=True)

    columns, rows = inverse_tables()
    model = model_facet.reshape(2 * F_ROWS, FACET)
    back = pl.pallas_call(
        functools.partial(pick_kernel, facets, cap),
        out_shape=tuple([jax.ShapeDtypeStruct((cap, SUB, LANES), jnp.bfloat16)] * facets),
        in_specs=[hbm(), vmem(), hbm(), hbm()],
        out_specs=tuple([vmem()] * facets),
        scratch_shapes=[
            pltpu.SMEM((WORDS,), jnp.int32),
            pltpu.VMEM((2 * SPAN + SUB, LANES), jnp.float32),
            pltpu.VMEM((2 * SUB, 2 * SUB), jnp.bfloat16),
            pltpu.VMEM((slots, SUB, LANES), jnp.bfloat16),
            pltpu.SMEM((slots + 1,), jnp.int32),
            copy_sems(3),
        ]
        + [pltpu.VMEM((2 * F_ROWS, LANES), jnp.float32)] * PICK_GROUP,
        compiler_params=params(),
        name="pick",
    )(listed, model, in_hbm(columns), in_hbm(rows))
    returned = [back[0]] + [partner(back[bit], "facet", bit) for bit in range(1, facets)]

    residual_vis = pl.pallas_call(
        functools.partial(degrid_kernel, facets),
        out_shape=jax.ShapeDtypeStruct((subs, 2, NV), jnp.float32),
        in_specs=[hbm()] * 4 + [vmem()] * facets,
        out_specs=vmem(),
        scratch_shapes=[
            pltpu.SMEM((subs,), jnp.int32),
            pltpu.SMEM((subs,), jnp.int32),
            pltpu.VMEM((subs, 2, NV), jnp.float32),
            pltpu.VMEM((subs, 2, NV), jnp.float32),
            pltpu.VMEM((facets, cap, SUB, LANES), jnp.bfloat16),
            pltpu.SMEM((facets,), jnp.int32),
            copy_sems(4),
        ],
        compiler_params=params(),
        name="degrid",
    )(*[in_hbm(value) for value in (facet_ids, vis_count, visibility, uv_coords)], *returned)

    every, rest, residual_vis = lax.optimization_barrier((every, rest, residual_vis))
    facet_image = pl.pallas_call(
        functools.partial(add_kernel, facets, chans, cap),
        out_shape=jax.ShapeDtypeStruct((shard, 2, FACET), jnp.float32),
        in_specs=[hbm(), hbm()],
        out_specs=hbm(),
        scratch_shapes=[
            pltpu.SMEM((total,), jnp.int32),
            pltpu.VMEM((total, shard, LANES), jnp.bfloat16),
            pltpu.VMEM((shard, 2, FACET), jnp.float32),
            copy_sems(1 + PARTS),
            copy_sems(IMAGE_PARTS),
        ]
        + [pltpu.VMEM((shard, 2 * FACET + 3 * LANES), jnp.float32)] * CANVASES,
        compiler_params=params(),
        name="add",
    )(jnp.concatenate([every, rest]), recv.reshape(total, shard, LANES))
    return (facet_image[None], residual_vis)


def solution(mesh):
    in_specs = (
        P(("facet", "chan"), None, None),
        P(("facet", "chan"), None, None),
        P(("facet", "chan")),
        P(("facet", "chan"), None),
        P(("facet", "chan")),
        P(("facet", "chan")),
        P("facet", None, None, None),
    )
    out_specs = (P("facet", "chan", None, None), P(("facet", "chan"), None, None))
    return jax.shard_map(
        per_device, mesh=mesh, in_specs=in_specs, out_specs=out_specs, check_vma=False
    )
```

```python
import functools
import math

import jax
import jax.numpy as jnp
import numpy as np
from jax import lax
from jax.experimental import pallas as pl
from jax.experimental.pallas import tpu as pltpu
from jax.sharding import PartitionSpec as P

SUB = 64
FACET = 4096
F_ROWS = 128
NV = 512
LANES = 128
VALID_BIT = 1 << 20
GROUP = 4
WORDS = 128

SPAN = 3 * SUB
PICK_GROUP = 16
CANVASES = 2
PARTS = 4

VMEM_LIMIT = 48 * 1024 * 1024


FACET_AXES = ("fy", "fx")


def turned(facet, facets):
    side = math.isqrt(facets)
    return lax.rem(facet, side) * side + lax.div(facet, side)


def dft_arrays():
    index_line = np.arange(SUB)
    phase = (index_line[:, None] * index_line[None, :]) % SUB
    angle = (2.0 * math.pi * phase / SUB).astype(np.float32)
    cos_table = np.cos(angle) / np.float32(math.sqrt(SUB))
    sin_table = -np.sin(angle) / np.float32(math.sqrt(SUB))
    return cos_table.astype(np.float32), sin_table.astype(np.float32)


def forward_table():
    cos_table, sin_table = dft_arrays()
    right = np.concatenate(
        [np.concatenate([cos_table, sin_table], 1), np.concatenate([-sin_table, cos_table], 1)], 0
    )
    return jnp.asarray(right, jnp.bfloat16)


def inverse_tables():
    cos_table, sin_table = dft_arrays()
    sin_table = -sin_table
    columns = np.zeros((2 * SPAN + SUB, LANES), np.float32)
    columns[SPAN : SPAN + SUB] = np.concatenate([cos_table, sin_table], 1)
    rows = np.zeros((2 * SUB, 2 * SUB), np.float32)
    rows[:SUB, 0::2] = cos_table
    rows[:SUB, 1::2] = -sin_table
    rows[SUB:, 0::2] = sin_table
    rows[SUB:, 1::2] = cos_table
    columns = columns.astype(jnp.bfloat16).astype(np.float32)
    return jnp.asarray(columns), jnp.asarray(rows, jnp.bfloat16)


def gaussian(coord_row):
    pixel = lax.broadcasted_iota(jnp.int32, (SUB, NV), 0).astype(jnp.float32)
    delta = pixel - coord_row
    return jnp.exp(-(delta * delta))


def live_row(count):
    return lax.broadcasted_iota(jnp.int32, (1, NV), 1) < count


def start(copies, sems):
    started = [
        pltpu.make_async_copy(source, target, sems.at[number])
        for number, (source, target) in enumerate(copies)
    ]
    for copy in started:
        copy.start()
    return started


def fetch(copies, sems):
    for copy in start(copies, sems):
        copy.wait()


def next_slot(facet_ref, used_ref, sub):
    facet = facet_ref[sub]
    slot = used_ref[facet]
    used_ref[facet] = slot + 1
    return facet, slot


def clear_used(used_ref, facets):
    for facet in range(facets):
        used_ref[facet] = 0


def grid_kernel(
    facets, chans, facet_in, row_in, col_in, count_in, vis_in, coord_in, right_in, send_ref, *refs
):
    meta_refs, refs = refs[:facets], refs[facets:]
    facet_ref, row_ref, col_ref, count_ref, vis_ref, coord_ref, right_ref, *refs = refs
    stack_ref, half_ref, pad_ref, used_ref, where_ref, sems = refs
    me = lax.axis_index(FACET_AXES)
    cap = send_ref.shape[2]
    subs = vis_ref.shape[0]
    shard = F_ROWS // chans
    fetch(
        [
            (facet_in, facet_ref),
            (row_in, row_ref),
            (col_in, col_ref),
            (count_in, count_ref),
            (vis_in, vis_ref),
            (coord_in, coord_ref),
            (right_in, right_ref),
        ],
        sems,
    )
    clear_used(used_ref, facets)
    for index in range(facets * cap):
        where_ref[index] = 0
    for member in range(GROUP):
        pad_ref[member, :SUB, :] = jnp.zeros((SUB, LANES), jnp.float32)
        pad_ref[member, 2 * SUB :, :] = jnp.zeros((SUB, LANES), jnp.float32)
    low_lanes = lax.broadcasted_iota(jnp.int32, (SUB, LANES), 1) < SUB

    def grid_one(sub):
        kernel_u = gaussian(coord_ref[sub, 0:1, :]).astype(jnp.bfloat16)
        kernel_v = gaussian(coord_ref[sub, 1:2, :])
        live = live_row(count_ref[sub])
        spread = jnp.concatenate(
            [
                (jnp.where(live, vis_ref[sub, part : part + 1, :], 0.0) * kernel_v).astype(
                    jnp.bfloat16
                )
                for part in range(2)
            ],
            0,
        )
        gridded = lax.dot_general(
            kernel_u, spread, (((1,), (1,)), ((), ())), preferred_element_type=jnp.float32
        )
        swapped = pltpu.roll(gridded, SUB, 1)
        swapped = jnp.where(low_lanes, -swapped, swapped)
        stack_ref[sub] = jnp.concatenate([gridded, swapped], 0).astype(jnp.bfloat16)

    def grid_group(group, carry):
        for member in range(GROUP):
            grid_one(group * GROUP + member)
        return carry

    lax.fori_loop(0, subs // GROUP, grid_group, 0, unroll=True)
    for sub in range(subs):
        half_ref[sub * SUB : (sub + 1) * SUB, :] = jnp.dot(
            right_ref[:SUB, :], stack_ref[sub], preferred_element_type=jnp.float32
        ).astype(jnp.bfloat16)

    for group in range(subs // GROUP):
        base = group * GROUP
        patches = jnp.dot(
            half_ref[base * SUB : (base + GROUP) * SUB, :],
            right_ref[...],
            preferred_element_type=jnp.float32,
        )
        for member in range(GROUP):
            patch = patches[member * SUB : (member + 1) * SUB]
            rolled = pltpu.roll(patch, col_ref[base + member] & (LANES - 1), 1)
            pad_ref[member, SUB : 2 * SUB, :] = rolled
        for member in range(GROUP):
            sub = base + member
            facet, slot = next_slot(facet_ref, used_ref, sub)
            row = row_ref[sub]
            placed = pad_ref[member, pl.ds(SUB - row, F_ROWS), :].astype(jnp.bfloat16)
            send_ref[:, turned(facet, facets), slot] = placed.reshape(chans, shard, LANES)
            where_ref[(facet ^ me) * cap + slot] = VALID_BIT + row * FACET + col_ref[sub]
    for number, meta_ref in enumerate(meta_refs):
        for slot in range(cap):
            meta_ref[slot] = where_ref[number * cap + slot]


def pick_kernel(facets, cap, *refs):
    meta_in, model_ref, columns_in, rows_in, *refs = refs
    back_refs, refs = refs[:facets], refs[facets:]
    meta_ref, columns_ref, rows_ref, back_ref, list_ref, sems, *wide_refs = refs
    slots = facets * cap
    loads = start([(meta_in, meta_ref), (columns_in, columns_ref), (rows_in, rows_ref)], sems)
    loads[0].wait()
    found = 0
    for source in range(facets):
        values = [meta_ref[source * cap + slot] for slot in range(cap)]
        for slot, packed in enumerate(values):
            list_ref[found] = (packed & (VALID_BIT - 1)) * slots + source * cap + slot
            found = found + (packed >= VALID_BIT).astype(jnp.int32)
    for load in loads[1:]:
        load.wait()
    low_lanes = lax.broadcasted_iota(jnp.int32, (SUB, LANES), 1) < SUB

    def columns_of(position, wide_ref):
        entry = list_ref[position]
        where = lax.div(entry, slots)
        col = where & (FACET - 1)
        block = jnp.minimum(lax.div(col, LANES), FACET // LANES - 2)
        slab = model_ref[:, pl.ds(pl.multiple_of(block * LANES, LANES), 2 * LANES)]
        table = columns_ref[pl.ds(SPAN - col + block * LANES, 2 * LANES), :]
        wide_ref[...] = jnp.dot(
            slab, table.astype(jnp.bfloat16), preferred_element_type=jnp.float32
        )
        return lax.rem(entry, slots), lax.div(where, FACET)

    def rows_of(row, wide_ref):
        half = wide_ref[pl.ds(2 * row, 2 * SUB), :].astype(jnp.bfloat16)
        return jnp.dot(rows_ref[...], half, preferred_element_type=jnp.float32)

    def finish(image):
        turned = pltpu.roll(image[SUB:], SUB, 1)
        return (image[:SUB] + jnp.where(low_lanes, -turned, turned)).astype(jnp.bfloat16)

    def windows(first, count):
        places = [
            columns_of(jnp.minimum(first + member, found - 1), wide_refs[member])
            for member in range(count)
        ]
        images = [rows_of(row, wide_refs[member]) for member, (_, row) in enumerate(places)]
        images = [finish(image) for image in images]
        for (index, _), image in zip(places, images):
            back_ref[index] = image

    def one_group(group, carry):
        windows(group * PICK_GROUP, PICK_GROUP)
        return carry

    half = PICK_GROUP // 2
    whole = lax.div(found, PICK_GROUP)
    rest = found - whole * PICK_GROUP
    lax.fori_loop(0, whole, one_group, 0)
    pl.when(rest > half)(lambda: windows(whole * PICK_GROUP, PICK_GROUP))
    pl.when((rest > 0) & (rest <= half))(lambda: windows(whole * PICK_GROUP, half))
    for number in range(facets):
        back_refs[number][...] = back_ref[number * cap : (number + 1) * cap]


def add_kernel(
    facets, chans, cap, meta_in, recv_in, image_ref, meta_ref, recv_ref, sems, *canvas_refs
):
    shard = F_ROWS // chans
    facet, chan = lax.axis_index(FACET_AXES), lax.axis_index("chan")
    span = chans // PARTS
    group = span * facets * cap
    groups = [pl.ds((number ^ lax.div(chan, span)) * group, group) for number in range(PARTS)]
    loads = start(
        [(meta_in, meta_ref)] + [(recv_in.at[part], recv_ref.at[part]) for part in groups], sems
    )
    for canvas_ref in canvas_refs:
        canvas_ref[...] = jnp.zeros_like(canvas_ref)
    loads[0].wait()
    lanes = lax.broadcasted_iota(jnp.int32, (shard, LANES), 1)
    within = lanes & (SUB - 1)

    def load(packed, index):
        col = jnp.where(packed >= VALID_BIT, packed & (FACET - 1), FACET + SUB)
        shift = col & (SUB - 1)
        turned = recv_ref[index].astype(jnp.float32)
        near = jnp.where(within >= shift, turned, 0.0)
        return lax.div(col, SUB) * LANES, near, jnp.where(within >= shift, 0.0, turned)

    def one_source(source, carry):
        number = lax.div(source, facets)
        first = ((number ^ chan) * facets + turned((source & (facets - 1)) ^ facet, facets)) * cap
        place = source * cap
        packs = [meta_ref[place + slot] for slot in range(cap)]
        loaded = [load(packed, first + slot) for slot, packed in enumerate(packs)]
        for slot, (start, near, far) in enumerate(loaded):
            canvas_ref = canvas_refs[slot % CANVASES]
            place = pl.ds(pl.multiple_of(start, LANES), 2 * LANES)
            canvas_ref[:, place] += jnp.concatenate([near, far], 1)
        return carry

    sources = span * facets
    for number in range(PARTS):
        loads[1 + number].wait()
        lax.fori_loop(number * sources, (number + 1) * sources, one_source, 0, unroll=8)
    for block in range(FACET // LANES):
        first, second = [
            sum(ref[:, (2 * block + half) * LANES : (2 * block + half + 1) * LANES] for ref in canvas_refs)
            for half in range(2)
        ]
        place = slice(block * LANES, (block + 1) * LANES)
        image_ref[:, 0, place] = jnp.where(lanes < SUB, first, second)
        image_ref[:, 1, place] = pltpu.roll(jnp.where(lanes < SUB, second, first), SUB, 1)


def degrid_kernel(facets, facet_in, count_in, vis_in, coord_in, *refs):
    back_in, refs = refs[:facets], refs[facets:]
    out_ref, facet_ref, count_ref, vis_ref, coord_ref, back_ref, used_ref, sems = refs
    subs = vis_ref.shape[0]
    loads = start(
        [
            (facet_in, facet_ref),
            (count_in, count_ref),
            (vis_in, vis_ref),
            (coord_in, coord_ref),
        ],
        sems,
    )
    for number in range(facets):
        back_ref[number] = back_in[number][...]
    for load in loads:
        load.wait()
    me = lax.axis_index(FACET_AXES)
    clear_used(used_ref, facets)
    low_lanes = lax.broadcasted_iota(jnp.int32, (SUB, LANES), 1) < SUB

    def one_group(group, carry):
        for member in range(GROUP):
            sub = group * GROUP + member
            facet, slot = next_slot(facet_ref, used_ref, sub)
            kernel_u = gaussian(coord_ref[sub, 0:1, :]).astype(jnp.bfloat16).astype(jnp.float32)
            kernel_v = gaussian(coord_ref[sub, 1:2, :]).astype(jnp.bfloat16)
            grid = back_ref[facet ^ me, slot].astype(jnp.float32)
            split = jnp.concatenate(
                [jnp.where(low_lanes, grid, 0.0), jnp.where(low_lanes, 0.0, grid)], 0
            ).astype(jnp.bfloat16)
            lines = jnp.dot(
                split,
                jnp.concatenate([kernel_v, kernel_v], 0),
                preferred_element_type=jnp.float32,
            )
            live = live_row(count_ref[sub])
            for part in range(2):
                predicted = jnp.sum(
                    lines[part * SUB : (part + 1) * SUB] * kernel_u, 0, keepdims=True
                )
                seen = vis_ref[sub, part : part + 1, :]
                out_ref[sub, part : part + 1, :] = jnp.where(live, seen - predicted, 0.0)
        return carry

    lax.fori_loop(0, subs // GROUP, one_group, 0, unroll=2)


def smem():
    return pl.BlockSpec(memory_space=pltpu.SMEM)


def vmem():
    return pl.BlockSpec(memory_space=pltpu.VMEM)


def hbm():
    return pl.BlockSpec(memory_space=pltpu.HBM)


def params():
    return pltpu.CompilerParams(vmem_limit_bytes=VMEM_LIMIT)


def copy_sems(count):
    return pltpu.SemaphoreType.DMA((count,))


def in_hbm(values):
    return pltpu.with_memory_space_constraint(values, pltpu.HBM)


def partner(values, axis, bit):
    return lax.ppermute(
        values, axis, [(index, index ^ bit) for index in range(lax.axis_size(axis))]
    )


def per_device(
    visibility, uv_coords, vis_count, subgrid_facet, row_offset, col_offset, model_facet
):
    facets = lax.axis_size(FACET_AXES)
    chans = lax.axis_size("chan")
    subs = visibility.shape[0]
    cap = max(2, 2 * subs // facets)
    shard = F_ROWS // chans
    slots = facets * cap
    total = slots * chans
    facet_ids = subgrid_facet[:, 0]

    grid_inputs = (
        facet_ids, row_offset, col_offset, vis_count, visibility, uv_coords, forward_table()
    )
    send, *metas = pl.pallas_call(
        functools.partial(grid_kernel, facets, chans),
        out_shape=tuple(
            [jax.ShapeDtypeStruct((chans, facets, cap, shard, LANES), jnp.bfloat16)]
            + [jax.ShapeDtypeStruct((WORDS,), jnp.int32)] * facets
        ),
        in_specs=[hbm()] * 7,
        out_specs=tuple([vmem()] + [smem()] * facets),
        scratch_shapes=[
            pltpu.SMEM((subs,), jnp.int32),
            pltpu.SMEM((subs,), jnp.int32),
            pltpu.SMEM((subs,), jnp.int32),
            pltpu.SMEM((subs,), jnp.int32),
            pltpu.VMEM((subs, 2, NV), jnp.float32),
            pltpu.VMEM((subs, 2, NV), jnp.float32),
            pltpu.VMEM((LANES, LANES), jnp.bfloat16),
            pltpu.VMEM((subs, LANES, LANES), jnp.bfloat16),
            pltpu.VMEM((subs * SUB, LANES), jnp.bfloat16),
            pltpu.VMEM((GROUP, 3 * SUB, LANES), jnp.float32),
            pltpu.SMEM((facets,), jnp.int32),
            pltpu.SMEM((slots,), jnp.int32),
            copy_sems(7),
        ],
        compiler_params=params(),
        name="grid",
    )(*[in_hbm(value) for value in grid_inputs])
    metas = metas[:1] + [partner(metas[bit], FACET_AXES, bit) for bit in range(1, facets)]
    mine = jnp.concatenate([values[:cap] for values in metas])
    listed = jnp.pad(mine, (0, WORDS - slots))
    every = mine
    bit = 1
    while 2 * bit < chans:
        every = jnp.concatenate([every, partner(every, "chan", bit)])
        bit *= 2
    rest = partner(every, "chan", bit)

    send, model_facet = lax.optimization_barrier((send, model_facet))
    send = send.reshape(chans * facets, cap, shard, LANES)
    recv = lax.all_to_all(send, ("chan", "fx", "fy"), split_axis=0, concat_axis=0, tiled=True)

    columns, rows = inverse_tables()
    model = model_facet.reshape(2 * F_ROWS, FACET)
    back = pl.pallas_call(
        functools.partial(pick_kernel, facets, cap),
        out_shape=tuple([jax.ShapeDtypeStruct((cap, SUB, LANES), jnp.bfloat16)] * facets),
        in_specs=[hbm(), vmem(), hbm(), hbm()],
        out_specs=tuple([vmem()] * facets),
        scratch_shapes=[
            pltpu.SMEM((WORDS,), jnp.int32),
            pltpu.VMEM((2 * SPAN + SUB, LANES), jnp.float32),
            pltpu.VMEM((2 * SUB, 2 * SUB), jnp.bfloat16),
            pltpu.VMEM((slots, SUB, LANES), jnp.bfloat16),
            pltpu.SMEM((slots + 1,), jnp.int32),
            copy_sems(3),
        ]
        + [pltpu.VMEM((2 * F_ROWS, LANES), jnp.float32)] * PICK_GROUP,
        compiler_params=params(),
        name="pick",
    )(listed, model, in_hbm(columns), in_hbm(rows))
    returned = [back[0]] + [partner(back[bit], FACET_AXES, bit) for bit in range(1, facets)]

    residual_vis = pl.pallas_call(
        functools.partial(degrid_kernel, facets),
        out_shape=jax.ShapeDtypeStruct((subs, 2, NV), jnp.float32),
        in_specs=[hbm()] * 4 + [vmem()] * facets,
        out_specs=vmem(),
        scratch_shapes=[
            pltpu.SMEM((subs,), jnp.int32),
            pltpu.SMEM((subs,), jnp.int32),
            pltpu.VMEM((subs, 2, NV), jnp.float32),
            pltpu.VMEM((subs, 2, NV), jnp.float32),
            pltpu.VMEM((facets, cap, SUB, LANES), jnp.bfloat16),
            pltpu.SMEM((facets,), jnp.int32),
            copy_sems(4),
        ],
        compiler_params=params(),
        name="degrid",
    )(*[in_hbm(value) for value in (facet_ids, vis_count, visibility, uv_coords)], *returned)

    every, rest, residual_vis = lax.optimization_barrier((every, rest, residual_vis))
    facet_image = pl.pallas_call(
        functools.partial(add_kernel, facets, chans, cap),
        out_shape=jax.ShapeDtypeStruct((shard, 2, FACET), jnp.float32),
        in_specs=[hbm(), hbm()],
        out_specs=vmem(),
        scratch_shapes=[
            pltpu.SMEM((total,), jnp.int32),
            pltpu.VMEM((total, shard, LANES), jnp.bfloat16),
            copy_sems(1 + PARTS),
        ]
        + [pltpu.VMEM((shard, 2 * FACET + 3 * LANES), jnp.float32)] * CANVASES,
        compiler_params=params(),
        name="add",
    )(jnp.concatenate([every, rest]), recv.reshape(total, shard, LANES))
    return (facet_image[None], residual_vis)


def solution(mesh):
    side = math.isqrt(mesh.devices.shape[0])
    mesh = jax.sharding.Mesh(
        mesh.devices.reshape((side, side, -1)), FACET_AXES + ("chan",)
    )
    in_specs = (
        P(FACET_AXES + ("chan",), None, None),
        P(FACET_AXES + ("chan",), None, None),
        P(FACET_AXES + ("chan",)),
        P(FACET_AXES + ("chan",), None),
        P(FACET_AXES + ("chan",)),
        P(FACET_AXES + ("chan",)),
        P(FACET_AXES, None, None, None),
    )
    out_specs = (P(FACET_AXES, "chan", None, None), P(FACET_AXES + ("chan",), None, None))
    return jax.shard_map(
        per_device, mesh=mesh, in_specs=in_specs, out_specs=out_specs, check_vma=False
    )
```
